128 devices in a mesh: pp: 8 (over x_lo, z), ep: 16 (over y, x_hi, core).
Axes of the slice: x: 4 (x_hi: 2, x_lo: 2; x = x_hi * 2 + x_lo), y: 4, z: 4, core: 2. Of those that a mesh axis runs over, the one named last changes fastest.
Arguments:
- ahead_input: bfloat16 [8, 2048, 7168], P('pp', 'ep'), may hold values from -6 to 6
- ahead_expert: int32 [8, 2048], P('pp', 'ep'), may hold values from 0 to 3, as said below
- ahead_slot: int32 [8, 2048], P('pp', 'ep'), may hold values from 0 to 31, as said below
- ahead_gate: float32 [8, 2048], P('pp', 'ep'), may hold values from 0.25 to 2.5
- back_input: bfloat16 [8, 2048, 7168], P('pp', 'ep'), may hold values from -6 to 6
- back_cotangent: bfloat16 [8, 2048, 7168], P('pp', 'ep'), may hold values from -6 to 6
- back_expert: int32 [8, 2048], P('pp', 'ep'), may hold values from 0 to 3, as said below
- back_slot: int32 [8, 2048], P('pp', 'ep'), may hold values from 0 to 31, as said below
- back_gate: float32 [8, 2048], P('pp', 'ep'), may hold values from 0.25 to 2.5
- gate_weight: bfloat16 [8, 16, 7168, 256], P('pp', 'ep'), may hold values from -0.0625 to 0.0625
- up_weight: bfloat16 [8, 16, 7168, 256], P('pp', 'ep'), may hold values from -0.0625 to 0.0625
- down_weight: bfloat16 [8, 16, 256, 7168], P('pp', 'ep'), may hold values from -0.1875 to 0.1875
Outputs:
- ahead_output: bfloat16 [8, 2048, 7168], P('pp', 'ep')
- back_gradient: bfloat16 [8, 2048, 7168], P('pp', 'ep')
The draws below stay inside these ranges and needn't reach their ends.
Inputs may be any that keep to these rules, and one draw needn't show every extreme that they name: `ahead_expert`: within the rows of one device (each block of 128 tokens) of each rank, every expert is named by exactly 32 rows. `ahead_slot`: within the rows of one device, the rows that name one expert carry the slots 0 to 31, each once. `back_expert`: within the rows of one device (each block of 128 tokens) of each rank, every expert is named by exactly 32 rows. `back_slot`: within the rows of one device, the rows that name one expert carry the slots 0 to 31, each once.
All inputs are finite; a program needn't handle non-finite values.
Results may differ from the reference program's by a relative error of at most 0.0056.
Values may be sent and summed in bfloat16 or wider, within the bound.
No kernel may reach another device: no remote copies, remote signals or barrier semaphores. Data moves between devices by JAX's collectives and lax.ppermute only.
A program may use at most 192 MiB of HBM per device.

```python
import math
import jax
import jax.numpy as jnp
from jax import lax

D = 7168
HEXP = 1024
SLICES = 4
TOK_DEV = 128
HS = 256
EXPERTS = 4
CAP = 32
TOKENS = 2048
N_PP = 8
N_EP = 16


def routing(key, salt):
    folded = jax.random.fold_in(key, salt)
    scores = jax.random.randint(folded, (N_PP, N_EP, TOK_DEV), 0, 1048576)
    scores = scores * TOK_DEV + jnp.arange(TOK_DEV, dtype=jnp.int32)
    ordering = jnp.argsort(scores, axis=-1).astype(jnp.int32)
    return ((ordering // CAP).reshape(N_PP, TOKENS), (ordering % CAP).reshape(N_PP, TOKENS))


def draw_ahead_expert(key, part):
    return routing(key, 17)[0]


def draw_ahead_slot(key, part):
    return routing(key, 17)[1]


def draw_back_expert(key, part):
    return routing(key, 29)[0]


def draw_back_slot(key, part):
    return routing(key, 29)[1]


def block_scale(rng, dims, split, low, top_value):
    factor_of = 1.0
    for position, parts in split:
        steps = jax.random.uniform(jax.random.fold_in(jax.random.fold_in(rng, 6), position), (parts,), jnp.float32, low / len(split), top_value / len(split))
        factor_of = factor_of * jnp.repeat(jnp.exp(steps), dims[position] // parts).reshape((-1,) + (1,) * (len(dims) - 1 - position))
    return factor_of


def noise(own_key, extent, deviation, most, shards=(), held_as=jnp.bfloat16):
    drawn = jax.random.normal(own_key, extent, jnp.float32) * deviation
    if len(shards) > 0:
        drawn = block_scale(own_key, extent, shards, -0.22, 0.18) * drawn
    return jnp.clip(drawn, min=-most, max=most).astype(held_as)


def setup_inputs(seed: int = 0) -> dict:
    key_of = jax.random.split(jax.random.key(seed), 13)
    return {
        "ahead_input": noise(key_of[0], (N_PP, TOKENS, D), 1.0, 6.0, ((0, 8), (1, 16))),
        "ahead_expert": draw_ahead_expert(jax.random.fold_in(key_of[12], 71), 0),
        "ahead_slot": draw_ahead_slot(jax.random.fold_in(key_of[12], 71), 0),
        "ahead_gate": jnp.clip(jnp.exp(math.log(2.5) - 2.3025851 * jax.random.uniform(key_of[3], (N_PP, TOKENS), jnp.float32) ** block_scale(key_of[3], (N_PP, TOKENS), ((0, 8), (1, 16)), -0.2, 0.2)), 0.25, 2.5),
        "back_input": noise(key_of[4], (N_PP, TOKENS, D), 1.0, 6.0, ((0, 8), (1, 16))),
        "back_cotangent": noise(key_of[5], (N_PP, TOKENS, D), 1.0, 6.0, ((0, 8), (1, 16))),
        "back_expert": draw_back_expert(jax.random.fold_in(key_of[12], 71), 0),
        "back_slot": draw_back_slot(jax.random.fold_in(key_of[12], 71), 0),
        "back_gate": jnp.clip(jnp.exp(math.log(2.5) - 2.3025851 * jax.random.uniform(key_of[8], (N_PP, TOKENS), jnp.float32) ** block_scale(key_of[8], (N_PP, TOKENS), ((0, 8), (1, 16)), -0.2, 0.2)), 0.25, 2.5),
        "gate_weight": noise(key_of[9], (N_PP, N_EP, D, HS), D ** -0.5, 0.0625, ((0, 8), (1, 16))),
        "up_weight": noise(key_of[10], (N_PP, N_EP, D, HS), D ** -0.5, 0.0625, ((0, 8), (1, 16))),
        "down_weight": noise(key_of[11], (N_PP, N_EP, HS, D), HEXP ** -0.5, 0.1875, ((0, 8), (1, 16))),
    }


epsilon = 1e-06

def normalize_rows(inputs):
    values = inputs.astype(jnp.float32)
    scales = lax.rsqrt(lax.optimization_barrier(jnp.mean(values * values, axis=-1, keepdims=True)) + epsilon)
    return (values, scales)

def contract_last(left, right):
    return lax.dot_general(left, right, (((1,), (1,)), ((), ())), preferred_element_type=jnp.float32)

def slice_forward(rows, gate_part, up_part, down_part):
    gate_values = jnp.dot(rows[0], gate_part, preferred_element_type=jnp.float32)
    up_values = jnp.dot(rows[0], up_part, preferred_element_type=jnp.float32)
    hidden = (jax.nn.silu(gate_values) * up_values).astype(jnp.bfloat16)
    return jnp.dot(hidden, down_part, preferred_element_type=jnp.float32).astype(jnp.bfloat16)

def slice_backward(rows, gate_part, up_part, down_part):
    gate_values = jnp.dot(rows[0], gate_part, preferred_element_type=jnp.float32)
    up_values = jnp.dot(rows[0], up_part, preferred_element_type=jnp.float32)
    upstream = contract_last(rows[1], down_part)
    sigmoid_values = jax.nn.sigmoid(gate_values)
    gate_gradient = (upstream * up_values * sigmoid_values * (1.0 + gate_values * (1.0 - sigmoid_values))).astype(jnp.bfloat16)
    up_gradient = (upstream * gate_values * sigmoid_values).astype(jnp.bfloat16)
    result = contract_last(gate_gradient, gate_part) + contract_last(up_gradient, up_part)
    return result.astype(jnp.bfloat16)

def place_rows(rows, positions):
    empty = jnp.zeros((EXPERTS * N_EP * CAP, D), jnp.bfloat16)
    return empty.at[positions].set(rows).reshape(EXPERTS, N_EP * CAP, D)

def expert_partials(function, stacks, gate_weight, up_weight, down_weight):

    def one_device(operands):
        device, gate_part, up_part, down_part = operands
        rows = tuple((lax.dynamic_index_in_dim(stacked, device // SLICES, 0, keepdims=False) for stacked in stacks))
        return function(rows, gate_part, up_part, down_part)
    return lax.map(one_device, (jnp.arange(N_EP, dtype=jnp.int32), gate_weight, up_weight, down_weight))

def combine_back(partials, positions):
    summed = partials.astype(jnp.float32).reshape(EXPERTS, SLICES, N_EP * CAP, D).sum(axis=1)
    return summed.reshape(EXPERTS * N_EP * CAP, D)[positions]

def rank_work(operands):
    ahead_input, ahead_expert, ahead_slot, ahead_gate, back_input, back_cotangent, back_expert, back_slot, back_gate, gate_weight, up_weight, down_weight = operands
    sources = jnp.arange(TOKENS, dtype=jnp.int32) // TOK_DEV
    ahead_positions = ahead_expert * (N_EP * CAP) + sources * CAP + ahead_slot
    back_positions = back_expert * (N_EP * CAP) + sources * CAP + back_slot
    values_ahead, scales_ahead = normalize_rows(ahead_input)
    normed_ahead = (values_ahead * scales_ahead).astype(jnp.bfloat16)
    partials = expert_partials(slice_forward, (place_rows(normed_ahead, ahead_positions),), gate_weight, up_weight, down_weight)
    combined = combine_back(partials, ahead_positions)
    ahead_layer = (values_ahead + ahead_gate[:, None] * combined).astype(jnp.bfloat16)
    values_back, scales_back = normalize_rows(back_input)
    normed_back = (values_back * scales_back).astype(jnp.bfloat16)
    stacks = (place_rows(normed_back, back_positions), place_rows(back_cotangent, back_positions))
    back_partials = expert_partials(slice_backward, stacks, gate_weight, up_weight, down_weight)
    grad_normed = back_gate[:, None] * combine_back(back_partials, back_positions)
    inner_sum = lax.optimization_barrier(jnp.sum(grad_normed * values_back, axis=-1, keepdims=True))
    cubed = scales_back * scales_back * scales_back
    grad_layer = scales_back * grad_normed - cubed * values_back * inner_sum / D + back_cotangent.astype(jnp.float32)
    return (ahead_layer, grad_layer.astype(jnp.bfloat16))

def reference(ahead_input, ahead_expert, ahead_slot, ahead_gate, back_input, back_cotangent, back_expert, back_slot, back_gate, gate_weight, up_weight, down_weight):
    ahead_layer, grad_layer = lax.map(rank_work, (ahead_input, ahead_expert, ahead_slot, ahead_gate, back_input, back_cotangent, back_expert, back_slot, back_gate, gate_weight, up_weight, down_weight))
    return (jnp.roll(ahead_layer, 1, axis=0), jnp.roll(grad_layer, -1, axis=0))
```

```python
import jax
import jax.numpy as jnp
from jax import lax
from jax.sharding import PartitionSpec as P

EPSILON = 1e-06
NY, NX, NC = 4, 2, 2


def move(block, dpp=0, dy=0, dx=0, dc=0):
    npp = lax.axis_size("pp")
    nep = lax.axis_size("ep")
    route = []
    for r in range(npp):
        for y in range(NY):
            for x in range(NX):
                for c in range(NC):
                    source = r * nep + (y * NX + x) * NC + c
                    to = ((y + dy) % NY * NX + (x + dx) % NX) * NC + (c + dc) % NC
                    route.append((source, (r + dpp) % npp * nep + to))
    return lax.ppermute(block, ("pp", "ep"), route)


def pick(positions, rows, along_rows):
    n = positions.shape[0]
    index = lax.broadcasted_iota(jnp.int32, (n, n), 0 if along_rows else 1)
    held = positions[None, :] if along_rows else positions[:, None]
    chosen = (index == held).astype(jnp.bfloat16)
    return jnp.dot(chosen, rows, preferred_element_type=jnp.float32).astype(jnp.bfloat16)


def pick_scalars(positions, values):
    n = positions.shape[0]
    index = lax.broadcasted_iota(jnp.int32, (n, n), 0)
    return jnp.sum(jnp.where(index == positions[None, :], values[None, :], 0.0), axis=1, keepdims=True)


def normalize_rows(inputs):
    values = inputs.astype(jnp.float32)
    scales = lax.rsqrt(jnp.mean(values * values, axis=-1, keepdims=True) + EPSILON)
    return (values * scales).astype(jnp.bfloat16), scales


def contract_last(left, right):
    return lax.dot_general(
        left, right, (((1,), (1,)), ((), ())), preferred_element_type=jnp.float32
    )


def dot(left, right):
    return jnp.dot(left, right, preferred_element_type=jnp.float32)


def body(
    ahead_input,
    ahead_expert,
    ahead_slot,
    ahead_gate,
    back_input,
    back_cotangent,
    back_expert,
    back_slot,
    back_gate,
    gate_weight,
    up_weight,
    down_weight,
):
    tokens, features = ahead_input.shape[1:]
    cap = tokens // NY
    y = lax.axis_index("ep") // (NX * NC)

    def block(rows, k):
        return rows[k * cap : (k + 1) * cap]

    ahead_positions = ((ahead_expert[0] - y + NY) % NY) * cap + ahead_slot[0]
    back_positions = ((back_expert[0] - y + NY) % NY) * cap + back_slot[0]

    far_cotangent = move(back_cotangent[0], dx=1)
    far_positions = move(back_positions, dx=1)
    gate_far, up_far, down_far = (
        move(gate_weight[0, 0], dc=1),
        move(up_weight[0, 0], dc=1),
        move(down_weight[0, 0], dc=1),
    )

    def along_y(rows):
        return jnp.concatenate(
            [block(rows, 0)] + [move(block(rows, k), dy=k) for k in range(1, NY)], axis=0
        )

    ahead_sorted = pick(ahead_positions, ahead_input[0], True)
    normed_ahead, _ = normalize_rows(ahead_sorted)
    ahead_near = along_y(normed_ahead)
    ahead_far = move(ahead_near, dx=1)
    back_sorted = pick(back_positions, back_input[0], True)
    normed_back, scales_back = normalize_rows(back_sorted)
    back_near = along_y(normed_back)
    back_far = move(back_near, dx=1)

    gate_part = jnp.concatenate([gate_weight[0, 0], gate_far], axis=1)
    up_part = jnp.concatenate([up_weight[0, 0], up_far], axis=1)
    down_part = jnp.concatenate([down_weight[0, 0], down_far], axis=0)

    cotangent_sorted = pick(back_positions, back_cotangent[0], True)
    far_sorted = pick(far_positions, far_cotangent, True)
    pairs = [jnp.concatenate([block(cotangent_sorted, k), block(far_sorted, k)], axis=0) for k in range(NY)]
    pairs = [pairs[0]] + [move(pairs[k], dy=k) for k in range(1, NY)]
    cotangent_rows = jnp.concatenate([p[:cap] for p in pairs] + [p[cap:] for p in pairs], axis=0)

    rows = jnp.concatenate([ahead_near, ahead_far], axis=0)
    hidden = (jax.nn.silu(dot(rows, gate_part)) * dot(rows, up_part)).astype(jnp.bfloat16)
    ahead_partial = dot(hidden, down_part).astype(jnp.bfloat16)

    rows = jnp.concatenate([back_near, back_far], axis=0)
    gated, lifted = dot(rows, gate_part), dot(rows, up_part)
    upstream = contract_last(cotangent_rows, down_part)
    sig = jax.nn.sigmoid(gated)
    gate_gradient = (upstream * lifted * sig * (1.0 + gated * (1.0 - sig))).astype(jnp.bfloat16)
    up_gradient = (upstream * gated * sig).astype(jnp.bfloat16)
    back_partial = (
        contract_last(gate_gradient, gate_part) + contract_last(up_gradient, up_part)
    ).astype(jnp.bfloat16)

    def give_back(partial, finish, dpp):
        near, far = partial[:tokens], partial[tokens:]
        done = [None] * NY
        for k in (2, 1, 3, 0):
            crossed = move(block(far, k), dx=1)
            total = block(near, k).astype(jnp.float32) + crossed.astype(jnp.float32)
            if k:
                total = move(total.astype(jnp.bfloat16), dy=-k).astype(jnp.float32)
            done[k] = move(finish(k, total), dpp=dpp)
        return jnp.concatenate(done, axis=0)

    gates = pick_scalars(ahead_positions, ahead_gate[0])

    def finish_ahead(k, total):
        return (block(ahead_sorted, k).astype(jnp.float32) + block(gates, k) * total).astype(jnp.bfloat16)

    back_gates = pick_scalars(back_positions, back_gate[0])

    def finish_back(k, total):
        values, scales = block(back_sorted, k).astype(jnp.float32), block(scales_back, k)
        grad_normed = block(back_gates, k) * total
        inner_sum = jnp.sum(grad_normed * values, axis=-1, keepdims=True)
        cubed = scales * scales * scales
        grad_layer = (
            scales * grad_normed
            - cubed * values * inner_sum / features
            + block(cotangent_sorted, k).astype(jnp.float32)
        )
        return grad_layer.astype(jnp.bfloat16)

    ahead_output = give_back(ahead_partial, finish_ahead, 1)
    back_gradient = give_back(back_partial, finish_back, -1)
    ahead_output = pick(move(ahead_positions, dpp=1), ahead_output, False)
    back_gradient = pick(move(back_positions, dpp=-1), back_gradient, False)
    return (ahead_output[None], back_gradient[None])


def solution(mesh):
    placed = (
        P("pp", "ep", None),
        P("pp", "ep"),
        P("pp", "ep"),
        P("pp", "ep"),
        P("pp", "ep", None),
        P("pp", "ep", None),
        P("pp", "ep"),
        P("pp", "ep"),
        P("pp", "ep"),
        P("pp", "ep", None, None),
        P("pp", "ep", None, None),
        P("pp", "ep", None, None),
    )
    return jax.shard_map(
        body,
        mesh=mesh,
        in_specs=placed,
        out_specs=(P("pp", "ep", None), P("pp", "ep", None)),
        check_vma=False,
    )
```

```python
import functools

import jax
import jax.numpy as jnp
from jax import lax
from jax.experimental import pallas as pl
from jax.experimental.pallas import tpu as pltpu
from jax.sharding import PartitionSpec as P

EPSILON = 1e-06
NY, NX, NC = 4, 2, 2
ORDER = (1, 3, 2, 0)
WIDE = 1024
VMEM = pltpu.CompilerParams(vmem_limit_bytes=40 * 1024 * 1024)
LIGHT = pl.CostEstimate(flops=1000, bytes_accessed=1000, transcendentals=0)


def move(block, dpp=0, dy=0, dx=0, dc=0):
    npp = lax.axis_size("pp")
    nep = lax.axis_size("ep")
    route = []
    for r in range(npp):
        for y in range(NY):
            for x in range(NX):
                for c in range(NC):
                    source = r * nep + (y * NX + x) * NC + c
                    to = ((y + dy) % NY * NX + (x + dx) % NX) * NC + (c + dc) % NC
                    route.append((source, (r + dpp) % npp * nep + to))
    return lax.ppermute(block, ("pp", "ep"), route)


def after(value, *earlier):
    return lax.optimization_barrier((value, *earlier))[0]


def contract_last(left, right):
    return lax.dot_general(
        left, right, (((1,), (1,)), ((), ())), preferred_element_type=jnp.float32
    )


def dot(left, right):
    return jnp.dot(left, right, preferred_element_type=jnp.float32)


def one_hot(positions):
    n = positions.shape[-1]
    index = lax.broadcasted_iota(jnp.int32, (n, n), 0)
    return (index == positions).astype(jnp.bfloat16)


def whole(kernel, outs, *operands, scratch=()):
    return pl.pallas_call(
        kernel,
        out_shape=outs,
        in_specs=[pl.BlockSpec(memory_space=pltpu.VMEM)] * len(operands),
        out_specs=jax.tree.map(lambda _: pl.BlockSpec(memory_space=pltpu.VMEM), outs),
        scratch_shapes=scratch,
        compiler_params=VMEM,
        cost_estimate=LIGHT,
    )(*operands)


def table(rows, features):
    return jax.ShapeDtypeStruct((rows, features), jnp.bfloat16)


def norm_kernel(inputs, expert_order, back_order, normed, kept, scales):
    features = inputs.shape[1]
    to_experts, to_back = one_hot(expert_order[...]), one_hot(back_order[...])
    sums = jnp.zeros((inputs.shape[0], 1), jnp.float32)
    kept_sums = sums
    for j in range(0, features, WIDE):
        values = inputs[:, j : j + WIDE]
        wide = values.astype(jnp.float32)
        sums += jnp.sum(wide * wide, axis=1, keepdims=True)
        moved = dot(to_back, values)
        kept_sums += jnp.sum(moved * moved, axis=1, keepdims=True)
        kept[:, j : j + WIDE] = moved.astype(jnp.bfloat16)
    scale = lax.rsqrt(sums / features + EPSILON)
    scales[...] = lax.rsqrt(kept_sums / features + EPSILON)
    for j in range(0, features, WIDE):
        scaled = (inputs[:, j : j + WIDE].astype(jnp.float32) * scale).astype(jnp.bfloat16)
        normed[:, j : j + WIDE] = dot(to_experts, scaled).astype(jnp.bfloat16)


def norm(inputs, expert_order, back_order):
    rows, features = inputs.shape
    outs = (table(rows, features), table(rows, features), jax.ShapeDtypeStruct((rows, 1), jnp.float32))
    return whole(norm_kernel, outs, inputs, expert_order, back_order)


def pair_kernel(near, far, near_order, far_order, back_order, pairs, kept):
    features = near.shape[1]
    cap = near.shape[0] // NY
    to_near, to_far, to_back = one_hot(near_order[...]), one_hot(far_order[...]), one_hot(back_order[...])
    for j in range(0, features, WIDE):
        here = slice(j, j + WIDE)
        kept[:, here] = dot(to_back, near[:, here]).astype(jnp.bfloat16)
        one = dot(to_near, near[:, here]).astype(jnp.bfloat16)
        two = dot(to_far, far[:, here]).astype(jnp.bfloat16)
        for e in range(NY):
            pairs[2 * e * cap : (2 * e + 1) * cap, here] = one[e * cap : (e + 1) * cap]
            pairs[(2 * e + 1) * cap : (2 * e + 2) * cap, here] = two[e * cap : (e + 1) * cap]


def unpick_kernel(order, *refs):
    *parts, out = refs
    chosen = one_hot(order[...]).T
    for j in range(0, out.shape[1], WIDE):
        rows = jnp.concatenate([p[:, j : j + WIDE] for p in parts], axis=0)
        out[:, j : j + WIDE] = dot(chosen, rows).astype(jnp.bfloat16)


def unpick(order, parts):
    return whole(unpick_kernel, table(order.shape[1], parts[0].shape[1]), order, *parts)


def sum_kernel(near, far, *outs):
    start = 0
    for out in outs:
        here = slice(start, start + out.shape[0])
        for j in range(0, out.shape[1], WIDE):
            across = slice(j, j + WIDE)
            total = near[here, across].astype(jnp.float32) + far[here, across].astype(jnp.float32)
            out[:, across] = total.astype(jnp.bfloat16)
        start += out.shape[0]


def read_total(blocks, summed, across):
    if not summed:
        return jnp.concatenate([b[:, across] for b in blocks], axis=0).astype(jnp.float32)
    return sum(b[:, across].astype(jnp.float32) for b in blocks)


def ahead_kernel(first, summed, kept, gates, *refs):
    *blocks, out = refs
    here = slice(first, first + out.shape[0])
    for j in range(0, out.shape[1], WIDE):
        across = slice(j, j + WIDE)
        total = read_total(blocks, summed, across)
        out[:, across] = (kept[here, across].astype(jnp.float32) + gates[here] * total).astype(jnp.bfloat16)


def back_kernel(first, summed, kept, cotangent, scales, gates, *refs):
    *blocks, out, grads = refs
    rows, features = out.shape
    here = slice(first, first + rows)
    scale = scales[here]
    inner_sum = jnp.zeros((rows, 1), jnp.float32)
    for j in range(0, features, WIDE):
        across = slice(j, j + WIDE)
        grad_normed = gates[here] * read_total(blocks, summed, across)
        grads[:, across] = grad_normed
        inner_sum += jnp.sum(grad_normed * kept[here, across].astype(jnp.float32), axis=1, keepdims=True)
    cubed = scale * scale * scale
    for j in range(0, features, WIDE):
        across = slice(j, j + WIDE)
        values = kept[here, across].astype(jnp.float32)
        grad_layer = (
            scale * grads[:, across]
            - cubed * values * inner_sum / features
            + cotangent[here, across].astype(jnp.float32)
        )
        out[:, across] = grad_layer.astype(jnp.bfloat16)


def by_distance(place, held, turned):
    half = held.shape[0] // 2
    cap = half // NY
    for h in range(2):
        for i, k in enumerate(ORDER):
            start = pl.multiple_of(h * half + (place[0] - k + NY) % NY * cap, cap)
            turned[h * half + i * cap : h * half + (i + 1) * cap] = held[pl.ds(start, cap)]


def store_parts(result, outs):
    start = 0
    for out in outs:
        out[...] = result[start : start + out.shape[0]].astype(jnp.bfloat16)
        start += out.shape[0]


def forward_kernel(steps, place, near, far, g0, g1, u0, u1, d0, d1, *refs):
    *outs, gated, lifted, hidden, turned = refs
    step = pl.program_id(0)
    half = g0.shape[1]

    @pl.when(step == 0)
    def _():
        gated[...] = jnp.zeros_like(gated)
        lifted[...] = jnp.zeros_like(lifted)

    @pl.when(step < steps)
    def _():
        rows = jnp.concatenate([near[...], far[...]], axis=0)
        gated[:, :half] += dot(rows, g0[...])
        gated[:, half:] += dot(rows, g1[...])
        lifted[:, :half] += dot(rows, u0[...])
        lifted[:, half:] += dot(rows, u1[...])

    @pl.when(step == steps - 1)
    def _():
        hidden[...] = (jax.nn.silu(gated[...]) * lifted[...]).astype(jnp.bfloat16)
        by_distance(place, hidden, turned)

    @pl.when(step >= steps)
    def _():
        store_parts(dot(turned[:, :half], d0[...]) + dot(turned[:, half:], d1[...]), outs)


def backward_kernel(steps, place, near, far, pairs, g0, g1, u0, u1, d0, d1, *refs):
    *outs, gated, lifted, upstream, gate_gradient, up_gradient, turned_gate, turned_up = refs
    step = pl.program_id(0)
    half = g0.shape[1]
    tokens = near.shape[0]
    cap = tokens // NY

    @pl.when(step == 0)
    def _():
        gated[...] = jnp.zeros_like(gated)
        lifted[...] = jnp.zeros_like(lifted)
        upstream[...] = jnp.zeros_like(upstream)

    @pl.when(step < steps)
    def _():
        rows = jnp.concatenate([near[...], far[...]], axis=0)
        gated[:, :half] += dot(rows, g0[...])
        gated[:, half:] += dot(rows, g1[...])
        lifted[:, :half] += dot(rows, u0[...])
        lifted[:, half:] += dot(rows, u1[...])
        upstream[:, :half] += contract_last(pairs[...], d0[...])
        upstream[:, half:] += contract_last(pairs[...], d1[...])

    @pl.when(step == steps - 1)
    def _():
        for h in range(2):
            for q in range(NY):
                here = slice(h * tokens + q * cap, h * tokens + (q + 1) * cap)
                gate, lift = gated[here], lifted[here]
                up = upstream[(2 * q + h) * cap : (2 * q + h + 1) * cap]
                sig = jax.nn.sigmoid(gate)
                gate_gradient[here] = (up * lift * sig * (1.0 + gate * (1.0 - sig))).astype(jnp.bfloat16)
                up_gradient[here] = (up * gate * sig).astype(jnp.bfloat16)
        by_distance(place, gate_gradient, turned_gate)
        by_distance(place, up_gradient, turned_up)

    @pl.when(step >= steps)
    def _():
        result = contract_last(turned_gate[:, :half], g0[...]) + contract_last(turned_gate[:, half:], g1[...])
        result += contract_last(turned_up[:, :half], u0[...]) + contract_last(turned_up[:, half:], u1[...])
        store_parts(result, outs)


def through_expert(kernel, place, rows, weights, parts, twice, scratch):
    features = rows[0].shape[1]
    steps = features // WIDE
    first = lambda i: jnp.minimum(i, steps - 1)
    second = lambda i: jnp.maximum(i - steps, 0)
    both = lambda i: i % steps
    gate = [pl.BlockSpec((WIDE, w.shape[1]), lambda i: ((both if twice else first)(i), 0)) for w in weights[:4]]
    down = [pl.BlockSpec((w.shape[0], WIDE), lambda i: (0, (first if twice else second)(i))) for w in weights[4:]]
    return pl.pallas_call(
        functools.partial(kernel, steps),
        grid=(2 * steps,),
        out_shape=[table(n, features) for n in parts],
        in_specs=[pl.BlockSpec(memory_space=pltpu.SMEM)]
        + [pl.BlockSpec((r.shape[0], WIDE), lambda i: (0, first(i))) for r in rows]
        + gate
        + down,
        out_specs=[pl.BlockSpec((n, WIDE), lambda i: (0, second(i))) for n in parts],
        scratch_shapes=scratch,
        compiler_params=VMEM,
        cost_estimate=LIGHT,
    )(place, *rows, *weights)


def body(
    ahead_input,
    ahead_expert,
    ahead_slot,
    ahead_gate,
    back_input,
    back_cotangent,
    back_expert,
    back_slot,
    back_gate,
    gate_weight,
    up_weight,
    down_weight,
):
    tokens, features = ahead_input.shape[1:]
    cap = tokens // NY
    units = gate_weight.shape[3]
    y = lax.axis_index("ep") // (NX * NC)
    place = y.astype(jnp.int32)[None]

    def along_y(rows):
        shape = (NY, rows.shape[0] // NY, features)
        groups = [
            [(q * NX + x) * NC + c for q in range(NY)] for x in range(NX) for c in range(NC)
        ]
        return lax.all_to_all(
            rows.reshape(shape), "ep", 0, 0, axis_index_groups=groups, tiled=True
        ).reshape(rows.shape)

    def cross(rows, *earlier):
        return move(after(rows, *earlier) if earlier else rows, dx=1)

    def positions(expert, slot):
        distance = (expert[0] - y + NY) % NY
        turn = jnp.select([distance == k for k in ORDER], list(range(NY)))
        return (expert * cap + slot), (turn * cap + slot[0])[None]

    ahead_order, ahead_turn = positions(ahead_expert, ahead_slot)
    back_order, back_turn = positions(back_expert, back_slot)
    half = tokens // 2

    far_cotangent = cross(back_cotangent[0])
    far_order = move(back_order, dx=1)
    gate_far = move(gate_weight[0, 0], dc=1)
    up_far = move(up_weight[0, 0], dc=1)
    down_far = move(down_weight[0, 0], dc=1)
    weights = (gate_weight[0, 0], gate_far, up_weight[0, 0], up_far, down_weight[0, 0], down_far)
    ahead_places, back_places = move(ahead_turn, dpp=1), move(back_turn, dpp=-1)

    normed_ahead, ahead_kept, _ = norm(ahead_input[0], ahead_order, ahead_turn)
    ahead_near = along_y(normed_ahead)
    normed_back, back_kept, scales_back = norm(back_input[0], back_order, back_turn)
    back_near = along_y(after(normed_back, ahead_near, far_cotangent, far_order, ahead_places, back_places))

    ahead_far = cross(ahead_near)
    pairs, cotangent_kept = whole(
        pair_kernel,
        (table(2 * tokens, features), table(tokens, features)),
        after(back_cotangent[0], back_near),
        far_cotangent,
        back_order,
        far_order,
        back_turn,
    )
    back_far = cross(back_near, pairs, ahead_far)
    pairs = along_y(pairs)

    groups = (2 * cap, cap, cap)
    wide = lambda dtype: pltpu.VMEM((2 * tokens, 2 * units), dtype)
    partials = through_expert(
        forward_kernel,
        place,
        (ahead_near, ahead_far),
        weights,
        (*groups, *groups),
        False,
        [wide(jnp.float32)] * 2 + [wide(jnp.bfloat16)] * 2,
    )
    ahead_home, ahead_away = partials[:3], partials[3:]
    partials = through_expert(
        backward_kernel,
        after(place, *ahead_home),
        (back_near, back_far, pairs),
        weights,
        (*groups, *groups),
        True,
        [wide(jnp.float32)] * 3 + [wide(jnp.bfloat16)] * 4,
    )
    back_home, back_away = partials[:3], partials[3:]

    def to_owner(home, other, *first):
        blocks = whole(sum_kernel, [table(cap, features)] * (home.shape[0] // cap), home, other)
        return [move(b, dy=-k) for b, k in zip(blocks, first)]

    def in_turn(turn, values):
        chosen = lax.broadcasted_iota(jnp.int32, (tokens, tokens), 0) == turn
        return jnp.sum(jnp.where(chosen, values, 0.0), axis=1, keepdims=True)

    ahead_gates = in_turn(ahead_turn, ahead_gate)
    back_gates = in_turn(back_turn, back_gate)

    def finish_ahead(first, blocks, summed=False):
        rows = cap if summed else cap * len(blocks)
        kernel = functools.partial(ahead_kernel, first * cap, summed)
        return move(whole(kernel, table(rows, features), ahead_kept, ahead_gates, *blocks), dpp=1)

    def finish_back(first, blocks, summed=False):
        rows = cap if summed else cap * len(blocks)
        return move(
            whole(
                functools.partial(back_kernel, first * cap, summed),
                table(rows, features),
                back_kept,
                cotangent_kept,
                scales_back,
                back_gates,
                *blocks,
                scratch=[pltpu.VMEM((rows, features), jnp.float32)],
            ),
            dpp=-1,
        )

    ahead_0 = cross(ahead_away[0], pairs)
    back_0 = cross(back_away[0])
    ahead_sums = to_owner(after(ahead_home[0], back_home[0]), ahead_0, *ORDER[:2])
    back_1 = cross(back_away[1], ahead_0)
    back_sums = to_owner(back_home[0], back_0, *ORDER[:2])
    ahead_1 = cross(ahead_away[1], back_0, *ahead_sums)
    ahead_low = finish_ahead(0, ahead_sums)
    ahead_2 = cross(ahead_away[2], back_1)
    back_sum = to_owner(back_home[1], back_1, *ORDER[2:3])
    back_low = finish_back(0, back_sums)
    back_2 = cross(back_away[2], ahead_1, *back_sums)
    ahead_sum = to_owner(after(ahead_home[1], *back_sum), ahead_1, *ORDER[2:3])
    back_middle = finish_back(2, [after(back_sum[0], ahead_low)])
    ahead_middle = finish_ahead(2, [after(ahead_sum[0], ahead_low)])
    ahead_last = finish_ahead(3, [ahead_home[2], ahead_2], True)
    back_last = finish_back(3, [after(back_home[2], back_low), back_2], True)
    ahead_output = unpick(ahead_places, [ahead_low, ahead_middle, ahead_last])
    back_gradient = unpick(back_places, [back_low, back_middle, back_last])
    return (ahead_output[None], back_gradient[None])


def solution(mesh):
    placed = (
        P("pp", "ep", None),
        P("pp", "ep"),
        P("pp", "ep"),
        P("pp", "ep"),
        P("pp", "ep", None),
        P("pp", "ep", None),
        P("pp", "ep"),
        P("pp", "ep"),
        P("pp", "ep"),
        P("pp", "ep", None, None),
        P("pp", "ep", None, None),
        P("pp", "ep", None, None),
    )
    return jax.shard_map(
        body,
        mesh=mesh,
        in_specs=placed,
        out_specs=(P("pp", "ep", None), P("pp", "ep", None)),
        check_vma=False,
    )
```

```python
import functools

import jax
import jax.numpy as jnp
from jax import lax
from jax.experimental import pallas as pl
from jax.experimental.pallas import tpu as pltpu
from jax.sharding import PartitionSpec as P

EPSILON = 1e-06
NY, NX, NC = 4, 2, 2
ORDER = (1, 3, 2, 0)
WIDE = 1024
LANES = 128
VMEM = pltpu.CompilerParams(vmem_limit_bytes=40 * 1024 * 1024)
LIGHT = pl.CostEstimate(flops=1000, bytes_accessed=1000, transcendentals=0)


def move(block, dpp=0, dy=0, dx=0, dc=0):
    npp = lax.axis_size("pp")
    nep = lax.axis_size("ep")
    route = []
    for r in range(npp):
        for y in range(NY):
            for x in range(NX):
                for c in range(NC):
                    source = r * nep + (y * NX + x) * NC + c
                    to = ((y + dy) % NY * NX + (x + dx) % NX) * NC + (c + dc) % NC
                    route.append((source, (r + dpp) % npp * nep + to))
    return lax.ppermute(block, ("pp", "ep"), route)


def after(value, *earlier):
    return lax.optimization_barrier((value, *earlier))[0]


def contract_last(left, right):
    return lax.dot_general(
        left, right, (((1,), (1,)), ((), ())), preferred_element_type=jnp.float32
    )


def dot(left, right):
    return jnp.dot(left, right, preferred_element_type=jnp.float32)


def one_hot(positions):
    n = positions.shape[-1]
    index = lax.broadcasted_iota(jnp.int32, (n, n), 0)
    return (index == positions).astype(jnp.bfloat16)


def whole(kernel, outs, *operands, scratch=()):
    return pl.pallas_call(
        kernel,
        out_shape=outs,
        in_specs=[pl.BlockSpec(memory_space=pltpu.SMEM if o.shape == (1,) else pltpu.VMEM) for o in operands],
        out_specs=jax.tree.map(lambda _: pl.BlockSpec(memory_space=pltpu.VMEM), outs),
        scratch_shapes=scratch,
        compiler_params=VMEM,
        cost_estimate=LIGHT,
    )(*operands)


def table(rows, features):
    return jax.ShapeDtypeStruct((rows, features), jnp.bfloat16)


def norm_kernel(inputs, expert_order, back_order, normed, kept, scales):
    features = inputs.shape[1]
    to_experts, to_back = one_hot(expert_order[...]), one_hot(back_order[...])
    sums = jnp.zeros((inputs.shape[0], 1), jnp.float32)
    kept_sums = sums
    for j in range(0, features, WIDE):
        values = inputs[:, j : j + WIDE]
        wide = values.astype(jnp.float32)
        sums += jnp.sum(wide * wide, axis=1, keepdims=True)
        moved = dot(to_back, values)
        kept_sums += jnp.sum(moved * moved, axis=1, keepdims=True)
        kept[:, j : j + WIDE] = moved.astype(jnp.bfloat16)
    scale = lax.rsqrt(sums / features + EPSILON)
    scales[...] = lax.rsqrt(kept_sums / features + EPSILON)
    for j in range(0, features, WIDE):
        scaled = (inputs[:, j : j + WIDE].astype(jnp.float32) * scale).astype(jnp.bfloat16)
        normed[:, j : j + WIDE] = dot(to_experts, scaled).astype(jnp.bfloat16)


def norm(inputs, expert_order, back_order):
    rows, features = inputs.shape
    outs = (table(rows, features), table(rows, features), jax.ShapeDtypeStruct((rows, 1), jnp.float32))
    return whole(norm_kernel, outs, inputs, expert_order, back_order)


def pair_kernel(near, far, near_order, far_order, back_order, pairs, kept):
    features = near.shape[1]
    cap = near.shape[0] // NY
    to_near, to_far, to_back = one_hot(near_order[...]), one_hot(far_order[...]), one_hot(back_order[...])
    for j in range(0, features, WIDE):
        here = slice(j, j + WIDE)
        kept[:, here] = dot(to_back, near[:, here]).astype(jnp.bfloat16)
        one = dot(to_near, near[:, here]).astype(jnp.bfloat16)
        two = dot(to_far, far[:, here]).astype(jnp.bfloat16)
        for e in range(NY):
            pairs[2 * e * cap : (2 * e + 1) * cap, here] = one[e * cap : (e + 1) * cap]
            pairs[(2 * e + 1) * cap : (2 * e + 2) * cap, here] = two[e * cap : (e + 1) * cap]


def unpick_kernel(*refs):
    *parts, out = refs
    tokens, features = out.shape

    def rows(here):
        return jnp.concatenate([p[:, here] for p in parts], axis=0)

    token = rows(slice(features, features + LANES)).astype(jnp.float32)
    index = lax.broadcasted_iota(jnp.int32, (tokens, LANES), 1).astype(jnp.float32)
    chosen = (token == index).astype(jnp.bfloat16).T
    for j in range(0, features, WIDE):
        here = slice(j, j + WIDE)
        out[:, here] = dot(chosen, rows(here)).astype(jnp.bfloat16)


def unpick(parts, tokens, features):
    return whole(unpick_kernel, table(tokens, features), *parts)


def sum_kernel(near, far, *outs):
    start = 0
    for out in outs:
        here = slice(start, start + out.shape[0])
        for j in range(0, out.shape[1], WIDE):
            across = slice(j, j + WIDE)
            total = near[here, across].astype(jnp.float32) + far[here, across].astype(jnp.float32)
            out[:, across] = total.astype(jnp.bfloat16)
        start += out.shape[0]


def read_total(blocks, summed, across):
    if not summed:
        return jnp.concatenate([b[:, across] for b in blocks], axis=0).astype(jnp.float32)
    return sum(b[:, across].astype(jnp.float32) for b in blocks)


def ahead_kernel(first, summed, kept, gates, tokens, *refs):
    *blocks, out = refs
    rows, features = out.shape[0], kept.shape[1]
    here = slice(first, first + rows)
    out[:, features:] = jnp.broadcast_to(tokens[here], (rows, LANES)).astype(jnp.bfloat16)
    for j in range(0, features, WIDE):
        across = slice(j, j + WIDE)
        total = read_total(blocks, summed, across)
        out[:, across] = (kept[here, across].astype(jnp.float32) + gates[here] * total).astype(jnp.bfloat16)


def back_kernel(first, summed, kept, gates, tokens, cotangent, scales, *refs):
    *blocks, out, grads = refs
    rows, features = out.shape[0], kept.shape[1]
    here = slice(first, first + rows)
    scale = scales[here]
    out[:, features:] = jnp.broadcast_to(tokens[here], (rows, LANES)).astype(jnp.bfloat16)
    inner_sum = jnp.zeros((rows, 1), jnp.float32)
    for j in range(0, features, WIDE):
        across = slice(j, j + WIDE)
        grad_normed = gates[here] * read_total(blocks, summed, across)
        grads[:, across] = grad_normed
        inner_sum += jnp.sum(grad_normed * kept[here, across].astype(jnp.float32), axis=1, keepdims=True)
    cubed = scale * scale * scale
    for j in range(0, features, WIDE):
        across = slice(j, j + WIDE)
        values = kept[here, across].astype(jnp.float32)
        grad_layer = (
            scale * grads[:, across]
            - cubed * values * inner_sum / features
            + cotangent[here, across].astype(jnp.float32)
        )
        out[:, across] = grad_layer.astype(jnp.bfloat16)


def by_distance(place, held, turned):
    half = held.shape[0] // 2
    cap = half // NY
    for h in range(2):
        for i, k in enumerate(ORDER):
            start = pl.multiple_of(h * half + (place[0] - k + NY) % NY * cap, cap)
            turned[h * half + i * cap : h * half + (i + 1) * cap] = held[pl.ds(start, cap)]


def store_parts(result, outs):
    start = 0
    for out in outs:
        out[...] = result[start : start + out.shape[0]].astype(jnp.bfloat16)
        start += out.shape[0]


def forward_kernel(steps, place, near, far, g0, g1, u0, u1, d0, d1, *refs):
    *outs, gated, lifted, hidden, turned = refs
    step = pl.program_id(0)
    half = g0.shape[1]

    @pl.when(step == 0)
    def _():
        gated[...] = jnp.zeros_like(gated)
        lifted[...] = jnp.zeros_like(lifted)

    @pl.when(step < steps)
    def _():
        rows = jnp.concatenate([near[...], far[...]], axis=0)
        gated[:, :half] += dot(rows, g0[...])
        gated[:, half:] += dot(rows, g1[...])
        lifted[:, :half] += dot(rows, u0[...])
        lifted[:, half:] += dot(rows, u1[...])

    @pl.when(step == steps - 1)
    def _():
        hidden[...] = (jax.nn.silu(gated[...]) * lifted[...]).astype(jnp.bfloat16)
        by_distance(place, hidden, turned)

    @pl.when(step >= steps)
    def _():
        store_parts(dot(turned[:, :half], d0[...]) + dot(turned[:, half:], d1[...]), outs)


def backward_kernel(steps, place, near, far, pairs, g0, g1, u0, u1, d0, d1, *refs):
    *outs, gated, lifted, upstream, gate_gradient, up_gradient, turned_gate, turned_up = refs
    step = pl.program_id(0)
    half = g0.shape[1]
    tokens = near.shape[0]
    cap = tokens // NY

    @pl.when(step == 0)
    def _():
        gated[...] = jnp.zeros_like(gated)
        lifted[...] = jnp.zeros_like(lifted)
        upstream[...] = jnp.zeros_like(upstream)

    @pl.when(step < steps)
    def _():
        rows = jnp.concatenate([near[...], far[...]], axis=0)
        gated[:, :half] += dot(rows, g0[...])
        gated[:, half:] += dot(rows, g1[...])
        lifted[:, :half] += dot(rows, u0[...])
        lifted[:, half:] += dot(rows, u1[...])
        upstream[:, :half] += contract_last(pairs[...], d0[...])
        upstream[:, half:] += contract_last(pairs[...], d1[...])

    @pl.when(step == steps - 1)
    def _():
        for h in range(2):
            for q in range(NY):
                here = slice(h * tokens + q * cap, h * tokens + (q + 1) * cap)
                gate, lift = gated[here], lifted[here]
                up = upstream[(2 * q + h) * cap : (2 * q + h + 1) * cap]
                sig = jax.nn.sigmoid(gate)
                gate_gradient[here] = (up * lift * sig * (1.0 + gate * (1.0 - sig))).astype(jnp.bfloat16)
                up_gradient[here] = (up * gate * sig).astype(jnp.bfloat16)
        by_distance(place, gate_gradient, turned_gate)
        by_distance(place, up_gradient, turned_up)

    @pl.when(step >= steps)
    def _():
        result = contract_last(turned_gate[:, :half], g0[...]) + contract_last(turned_gate[:, half:], g1[...])
        result += contract_last(turned_up[:, :half], u0[...]) + contract_last(turned_up[:, half:], u1[...])
        store_parts(result, outs)


def through_expert(kernel, place, rows, weights, parts, twice, scratch):
    features = rows[0].shape[1]
    steps = features // WIDE
    first = lambda i: jnp.minimum(i, steps - 1)
    second = lambda i: jnp.maximum(i - steps, 0)
    both = lambda i: i % steps
    gate = [pl.BlockSpec((WIDE, w.shape[1]), lambda i: ((both if twice else first)(i), 0)) for w in weights[:4]]
    down = [pl.BlockSpec((w.shape[0], WIDE), lambda i: (0, (first if twice else second)(i))) for w in weights[4:]]
    return pl.pallas_call(
        functools.partial(kernel, steps),
        grid=(2 * steps,),
        out_shape=[table(n, features) for n in parts],
        in_specs=[pl.BlockSpec(memory_space=pltpu.SMEM)]
        + [pl.BlockSpec((r.shape[0], WIDE), lambda i: (0, first(i))) for r in rows]
        + gate
        + down,
        out_specs=[pl.BlockSpec((n, WIDE), lambda i: (0, second(i))) for n in parts],
        scratch_shapes=scratch,
        compiler_params=VMEM,
        cost_estimate=LIGHT,
    )(place, *rows, *weights)


def body(
    ahead_input,
    ahead_expert,
    ahead_slot,
    ahead_gate,
    back_input,
    back_cotangent,
    back_expert,
    back_slot,
    back_gate,
    gate_weight,
    up_weight,
    down_weight,
):
    tokens, features = ahead_input.shape[1:]
    cap = tokens // NY
    units = gate_weight.shape[3]
    y = lax.axis_index("ep") // (NX * NC)
    place = y.astype(jnp.int32)[None]

    def along_y(rows):
        shape = (NY, rows.shape[0] // NY, features)
        groups = [
            [(q * NX + x) * NC + c for q in range(NY)] for x in range(NX) for c in range(NC)
        ]
        return lax.all_to_all(
            rows.reshape(shape), "ep", 0, 0, axis_index_groups=groups, tiled=True
        ).reshape(rows.shape)

    def cross(rows, *earlier):
        return move(after(rows, *earlier) if earlier else rows, dx=1)

    def positions(expert, slot):
        distance = (expert[0] - y + NY) % NY
        turn = jnp.select([distance == k for k in ORDER], list(range(NY)))
        return (expert * cap + slot), (turn * cap + slot[0])[None]

    ahead_order, ahead_turn = positions(ahead_expert, ahead_slot)
    back_order, back_turn = positions(back_expert, back_slot)
    half = tokens // 2

    far_cotangent = cross(back_cotangent[0])
    far_order = move(back_order, dx=1)
    gate_far = move(gate_weight[0, 0], dc=1)
    up_far = move(up_weight[0, 0], dc=1)
    down_far = move(down_weight[0, 0], dc=1)
    weights = (gate_weight[0, 0], gate_far, up_weight[0, 0], up_far, down_weight[0, 0], down_far)

    normed_ahead, ahead_kept, _ = norm(ahead_input[0], ahead_order, ahead_turn)
    ahead_near = along_y(normed_ahead)
    normed_back, back_kept, scales_back = norm(back_input[0], back_order, back_turn)
    back_near = along_y(after(normed_back, ahead_near, far_cotangent, far_order))

    ahead_far = cross(ahead_near)
    pairs, cotangent_kept = whole(
        pair_kernel,
        (table(2 * tokens, features), table(tokens, features)),
        after(back_cotangent[0], back_near),
        far_cotangent,
        back_order,
        far_order,
        back_turn,
    )
    back_far = cross(back_near, pairs, ahead_far)
    pairs = along_y(pairs)

    ahead_groups, back_groups = (2 * cap, 2 * cap), (2 * cap, cap, cap)
    wide = lambda dtype: pltpu.VMEM((2 * tokens, 2 * units), dtype)
    partials = through_expert(
        forward_kernel,
        place,
        (ahead_near, ahead_far),
        weights,
        (*ahead_groups, *ahead_groups),
        False,
        [wide(jnp.float32)] * 2 + [wide(jnp.bfloat16)] * 2,
    )
    ahead_home, ahead_away = partials[:2], partials[2:]
    partials = through_expert(
        backward_kernel,
        after(place, *ahead_home),
        (back_near, back_far, pairs),
        weights,
        (*back_groups, *back_groups),
        True,
        [wide(jnp.float32)] * 3 + [wide(jnp.bfloat16)] * 4,
    )
    back_home, back_away = partials[:3], partials[3:]

    def to_owner(home, other, *first):
        blocks = whole(sum_kernel, [table(cap, features)] * (home.shape[0] // cap), home, other)
        return blocks[-1], [move(b, dy=-k) for b, k in zip(blocks, first)]

    def in_turn(turn, values):
        chosen = lax.broadcasted_iota(jnp.int32, (tokens, tokens), 0) == turn
        return jnp.sum(jnp.where(chosen, values, 0.0), axis=1, keepdims=True)

    ahead_gates = in_turn(ahead_turn, ahead_gate)
    back_gates = in_turn(back_turn, back_gate)

    token = jnp.arange(tokens, dtype=jnp.float32)[None]
    ahead_rows = (ahead_kept, ahead_gates, in_turn(ahead_turn, token))
    back_rows = (back_kept, back_gates, in_turn(back_turn, token), cotangent_kept, scales_back)

    def finish_ahead(first, blocks, summed=False):
        rows = cap if summed else cap * len(blocks)
        kernel = functools.partial(ahead_kernel, first * cap, summed)
        return whole(kernel, table(rows, features + LANES), *ahead_rows, *blocks)

    def finish_back(first, blocks, summed=False):
        rows = cap if summed else cap * len(blocks)
        return whole(
            functools.partial(back_kernel, first * cap, summed),
            table(rows, features + LANES),
            *back_rows,
            *blocks,
            scratch=[pltpu.VMEM((rows, features), jnp.float32)],
        )


    a0 = cross(ahead_away[0])
    b0 = cross(back_away[0], a0)
    b1 = cross(back_away[1])
    done, asum = to_owner(after(ahead_home[0], back_home[0]), a0, *ORDER[:2])
    done, bsum = to_owner(after(back_home[0], done), b0, *ORDER[:2])
    done, bsum2 = to_owner(after(back_home[1], done), b1, *ORDER[2:3])
    a1 = cross(ahead_away[1], b0, b1)
    ahead_low = finish_ahead(0, [after(asum[0], done), asum[1]])
    zA13 = move(ahead_low, dpp=1)
    back_low = finish_back(0, [after(bsum[0], ahead_low), bsum[1]])
    zB13 = move(back_low, dpp=-1)
    b2 = cross(back_away[2], b1)
    done = finish_back(2, [after(bsum2[0], back_low)])
    zB2 = move(done, dpp=-1)
    ahead_sum, ahead_own = whole(sum_kernel, [table(cap, features)] * 2, after(ahead_home[1], done), a1)
    asum2 = [move(ahead_sum, dy=-ORDER[2])]
    done = finish_back(3, [after(back_home[2], ahead_own, zB13), b2], True)
    zB0 = move(done, dpp=-1)
    done = finish_ahead(2, [after(asum2[0], done, zA13, b2), ahead_own])
    zA2 = move(done, dpp=1)
    ahead_output = unpick([after(zA13, done), zA2], tokens, features)
    back_gradient = unpick([zB13, zB2, zB0], tokens, features)
    return (ahead_output[None], back_gradient[None])


def solution(mesh):
    placed = (
        P("pp", "ep", None),
        P("pp", "ep"),
        P("pp", "ep"),
        P("pp", "ep"),
        P("pp", "ep", None),
        P("pp", "ep", None),
        P("pp", "ep"),
        P("pp", "ep"),
        P("pp", "ep"),
        P("pp", "ep", None, None),
        P("pp", "ep", None, None),
        P("pp", "ep", None, None),
    )
    return jax.shard_map(
        body,
        mesh=mesh,
        in_specs=placed,
        out_specs=(P("pp", "ep", None), P("pp", "ep", None)),
        check_vma=False,
    )
```

```python
import functools

import jax
import jax.numpy as jnp
from jax import lax
from jax.experimental import pallas as pl
from jax.experimental.pallas import tpu as pltpu
from jax.sharding import PartitionSpec as P

EPSILON = 1e-06
NY, NX, NC = 4, 2, 2
ORDER = (1, 3, 2, 0)
WIDE = 1024
SPAN = 3584
LANES = 128
VMEM = pltpu.CompilerParams(vmem_limit_bytes=40 * 1024 * 1024)
LIGHT = pl.CostEstimate(flops=1000, bytes_accessed=1000, transcendentals=0)


def move(block, dpp=0, dy=0, dx=0, dc=0):
    npp = lax.axis_size("pp")
    nep = lax.axis_size("ep")
    route = []
    for r in range(npp):
        for y in range(NY):
            for x in range(NX):
                for c in range(NC):
                    source = r * nep + (y * NX + x) * NC + c
                    to = ((y + dy) % NY * NX + (x + dx) % NX) * NC + (c + dc) % NC
                    route.append((source, (r + dpp) % npp * nep + to))
    return lax.ppermute(block, ("pp", "ep"), route)


def after(value, *earlier):
    return lax.optimization_barrier((value, *earlier))[0]


def contract_last(left, right):
    return lax.dot_general(
        left, right, (((1,), (1,)), ((), ())), preferred_element_type=jnp.float32
    )


def dot(left, right):
    return jnp.dot(left, right, preferred_element_type=jnp.float32)


def one_hot(positions):
    n = positions.shape[-1]
    index = lax.broadcasted_iota(jnp.int32, (n, n), 0)
    return (index == positions).astype(jnp.bfloat16)


def whole(kernel, outs, *operands, scratch=()):
    return pl.pallas_call(
        kernel,
        out_shape=outs,
        in_specs=[pl.BlockSpec(memory_space=pltpu.SMEM if o.shape == (1,) else pltpu.VMEM) for o in operands],
        out_specs=jax.tree.map(lambda _: pl.BlockSpec(memory_space=pltpu.VMEM), outs),
        scratch_shapes=scratch,
        compiler_params=VMEM,
        cost_estimate=LIGHT,
    )(*operands)


def table(rows, features):
    return jax.ShapeDtypeStruct((rows, features), jnp.bfloat16)


def norm_kernel(inputs, expert_order, back_order, normed, kept, scales):
    features = inputs.shape[1]
    to_experts, to_back = one_hot(expert_order[...]), one_hot(back_order[...])
    sums = jnp.zeros((inputs.shape[0], 1), jnp.float32)
    kept_sums = sums
    for j in range(0, features, WIDE):
        values = inputs[:, j : j + WIDE]
        wide = values.astype(jnp.float32)
        sums += jnp.sum(wide * wide, axis=1, keepdims=True)
        moved = dot(to_back, values)
        kept_sums += jnp.sum(moved * moved, axis=1, keepdims=True)
        kept[:, j : j + WIDE] = moved.astype(jnp.bfloat16)
    scale = lax.rsqrt(sums / features + EPSILON)
    scales[...] = lax.rsqrt(kept_sums / features + EPSILON)
    for j in range(0, features, WIDE):
        scaled = (inputs[:, j : j + WIDE].astype(jnp.float32) * scale).astype(jnp.bfloat16)
        normed[:, j : j + WIDE] = dot(to_experts, scaled).astype(jnp.bfloat16)


def norm(inputs, expert_order, back_order):
    rows, features = inputs.shape
    outs = (table(rows, features), table(rows, features), jax.ShapeDtypeStruct((rows, 1), jnp.float32))
    return whole(norm_kernel, outs, inputs, expert_order, back_order)


def pair_kernel(near, far, near_order, far_order, back_order, pairs, kept):
    features = near.shape[1]
    cap = near.shape[0] // NY
    to_near, to_far, to_back = one_hot(near_order[...]), one_hot(far_order[...]), one_hot(back_order[...])
    for j in range(0, features, WIDE):
        here = slice(j, j + WIDE)
        kept[:, here] = dot(to_back, near[:, here]).astype(jnp.bfloat16)
        one = dot(to_near, near[:, here]).astype(jnp.bfloat16)
        two = dot(to_far, far[:, here]).astype(jnp.bfloat16)
        for e in range(NY):
            pairs[2 * e * cap : (2 * e + 1) * cap, here] = one[e * cap : (e + 1) * cap]
            pairs[(2 * e + 1) * cap : (2 * e + 2) * cap, here] = two[e * cap : (e + 1) * cap]


def unpick_kernel(*refs):
    *parts, out = refs
    tokens, features = out.shape

    def rows(here):
        return jnp.concatenate([p[:, here] for p in parts], axis=0)

    token = rows(slice(features, features + LANES)).astype(jnp.float32)
    index = lax.broadcasted_iota(jnp.int32, (tokens, LANES), 1).astype(jnp.float32)
    chosen = (token == index).astype(jnp.bfloat16).T
    for j in range(0, features, WIDE):
        here = slice(j, j + WIDE)
        out[:, here] = dot(chosen, rows(here)).astype(jnp.bfloat16)


def unpick(parts, tokens, features):
    return whole(unpick_kernel, table(tokens, features), *parts)


def sum_kernel(near, far, *outs):
    start = 0
    for out in outs:
        here = slice(start, start + out.shape[0])
        for j in range(0, out.shape[1], WIDE):
            across = slice(j, j + WIDE)
            total = near[here, across].astype(jnp.float32) + far[here, across].astype(jnp.float32)
            out[:, across] = total.astype(jnp.bfloat16)
        start += out.shape[0]


def read_total(blocks, summed, across):
    if not summed:
        return jnp.concatenate([b[:, across] for b in blocks], axis=0).astype(jnp.float32)
    return sum(b[:, across].astype(jnp.float32) for b in blocks)


def ahead_kernel(first, summed, kept, gates, tokens, *refs):
    *blocks, out = refs
    rows, features = out.shape[0], kept.shape[1]
    here = slice(first, first + rows)
    out[:, features:] = jnp.broadcast_to(tokens[here], (rows, LANES)).astype(jnp.bfloat16)
    for j in range(0, features, WIDE):
        across = slice(j, j + WIDE)
        total = read_total(blocks, summed, across)
        out[:, across] = (kept[here, across].astype(jnp.float32) + gates[here] * total).astype(jnp.bfloat16)


def back_kernel(first, summed, kept, gates, tokens, cotangent, scales, *refs):
    *blocks, out, grads = refs
    rows, features = out.shape[0], kept.shape[1]
    here = slice(first, first + rows)
    scale = scales[here]
    out[:, features:] = jnp.broadcast_to(tokens[here], (rows, LANES)).astype(jnp.bfloat16)
    inner_sum = jnp.zeros((rows, 1), jnp.float32)
    for j in range(0, features, WIDE):
        across = slice(j, j + WIDE)
        grad_normed = gates[here] * read_total(blocks, summed, across)
        grads[:, across] = grad_normed
        inner_sum += jnp.sum(grad_normed * kept[here, across].astype(jnp.float32), axis=1, keepdims=True)
    cubed = scale * scale * scale
    for j in range(0, features, WIDE):
        across = slice(j, j + WIDE)
        values = kept[here, across].astype(jnp.float32)
        grad_layer = (
            scale * grads[:, across]
            - cubed * values * inner_sum / features
            + cotangent[here, across].astype(jnp.float32)
        )
        out[:, across] = grad_layer.astype(jnp.bfloat16)


def by_distance(place, held, turned):
    half = held.shape[0] // 2
    cap = half // NY
    for h in range(2):
        for i, k in enumerate(ORDER):
            start = pl.multiple_of(h * half + (place[0] - k + NY) % NY * cap, cap)
            turned[h * half + i * cap : h * half + (i + 1) * cap] = held[pl.ds(start, cap)]


def store_parts(result, outs):
    start = 0
    for out in outs:
        out[...] = result[start : start + out.shape[0]].astype(jnp.bfloat16)
        start += out.shape[0]


def forward_kernel(steps, place, near, far, g0, g1, u0, u1, d0, d1, *refs):
    *outs, gated, lifted, hidden, turned = refs
    step = pl.program_id(0)
    half = g0.shape[1]

    @pl.when(step == 0)
    def _():
        gated[...] = jnp.zeros_like(gated)
        lifted[...] = jnp.zeros_like(lifted)

    @pl.when(step < steps)
    def _():
        rows = jnp.concatenate([near[...], far[...]], axis=0)
        gated[:, :half] += dot(rows, g0[...])
        gated[:, half:] += dot(rows, g1[...])
        lifted[:, :half] += dot(rows, u0[...])
        lifted[:, half:] += dot(rows, u1[...])

    @pl.when(step == steps - 1)
    def _():
        hidden[...] = (jax.nn.silu(gated[...]) * lifted[...]).astype(jnp.bfloat16)
        by_distance(place, hidden, turned)

    @pl.when(step >= steps)
    def _():
        store_parts(dot(turned[:, :half], d0[...]) + dot(turned[:, half:], d1[...]), outs)


def backward_kernel(steps, place, near, far, pairs, g0, g1, u0, u1, d0, d1, *refs):
    *outs, gated, lifted, upstream, gate_gradient, up_gradient, turned_gate, turned_up = refs
    step = pl.program_id(0)
    half = g0.shape[1]
    tokens = near.shape[0]
    cap = tokens // NY

    @pl.when(step == 0)
    def _():
        gated[...] = jnp.zeros_like(gated)
        lifted[...] = jnp.zeros_like(lifted)
        upstream[...] = jnp.zeros_like(upstream)

    @pl.when(step < steps)
    def _():
        rows = jnp.concatenate([near[...], far[...]], axis=0)
        gated[:, :half] += dot(rows, g0[...])
        gated[:, half:] += dot(rows, g1[...])
        lifted[:, :half] += dot(rows, u0[...])
        lifted[:, half:] += dot(rows, u1[...])
        upstream[:, :half] += contract_last(pairs[...], d0[...])
        upstream[:, half:] += contract_last(pairs[...], d1[...])

    @pl.when(step == steps - 1)
    def _():
        for h in range(2):
            for q in range(NY):
                here = slice(h * tokens + q * cap, h * tokens + (q + 1) * cap)
                gate, lift = gated[here], lifted[here]
                up = upstream[(2 * q + h) * cap : (2 * q + h + 1) * cap]
                sig = jax.nn.sigmoid(gate)
                gate_gradient[here] = (up * lift * sig * (1.0 + gate * (1.0 - sig))).astype(jnp.bfloat16)
                up_gradient[here] = (up * gate * sig).astype(jnp.bfloat16)
        by_distance(place, gate_gradient, turned_gate)
        by_distance(place, up_gradient, turned_up)

    @pl.when(step >= steps)
    def _():
        result = contract_last(turned_gate[:, :half], g0[...]) + contract_last(turned_gate[:, half:], g1[...])
        result += contract_last(turned_up[:, :half], u0[...]) + contract_last(turned_up[:, half:], u1[...])
        store_parts(result, outs)


def through_expert(kernel, place, rows, weights, parts, twice, scratch):
    features = rows[0].shape[1]
    steps = features // SPAN
    first = lambda i: jnp.minimum(i, steps - 1)
    second = lambda i: jnp.maximum(i - steps, 0)
    both = lambda i: i % steps
    gate = [pl.BlockSpec((SPAN, w.shape[1]), lambda i: ((both if twice else first)(i), 0)) for w in weights[:4]]
    down = [pl.BlockSpec((w.shape[0], SPAN), lambda i: (0, (first if twice else second)(i))) for w in weights[4:]]
    return pl.pallas_call(
        functools.partial(kernel, steps),
        grid=(2 * steps,),
        out_shape=[table(n, features) for n in parts],
        in_specs=[pl.BlockSpec(memory_space=pltpu.SMEM)]
        + [pl.BlockSpec((r.shape[0], SPAN), lambda i: (0, first(i))) for r in rows]
        + gate
        + down,
        out_specs=[pl.BlockSpec((n, SPAN), lambda i: (0, second(i))) for n in parts],
        scratch_shapes=scratch,
        compiler_params=VMEM,
        cost_estimate=LIGHT,
    )(place, *rows, *weights)


def body(
    ahead_input,
    ahead_expert,
    ahead_slot,
    ahead_gate,
    back_input,
    back_cotangent,
    back_expert,
    back_slot,
    back_gate,
    gate_weight,
    up_weight,
    down_weight,
):
    tokens, features = ahead_input.shape[1:]
    cap = tokens // NY
    units = gate_weight.shape[3]
    y = lax.axis_index("ep") // (NX * NC)
    place = y.astype(jnp.int32)[None]

    def along_y(rows):
        shape = (NY, rows.shape[0] // NY, features)
        groups = [
            [(q * NX + x) * NC + c for q in range(NY)] for x in range(NX) for c in range(NC)
        ]
        return lax.all_to_all(
            rows.reshape(shape), "ep", 0, 0, axis_index_groups=groups, tiled=True
        ).reshape(rows.shape)

    def cross(rows, *earlier):
        return move(after(rows, *earlier) if earlier else rows, dx=1)

    def positions(expert, slot):
        distance = (expert[0] - y + NY) % NY
        turn = jnp.select([distance == k for k in ORDER], list(range(NY)))
        return (expert * cap + slot), (turn * cap + slot[0])[None]

    ahead_order, ahead_turn = positions(ahead_expert, ahead_slot)
    back_order, back_turn = positions(back_expert, back_slot)
    half = tokens // 2

    far_cotangent = cross(back_cotangent[0])
    far_order = move(back_order, dx=1)
    gate_far = move(gate_weight[0, 0], dc=1)
    up_far = move(up_weight[0, 0], dc=1)
    down_far = move(down_weight[0, 0], dc=1)
    weights = (gate_weight[0, 0], gate_far, up_weight[0, 0], up_far, down_weight[0, 0], down_far)

    normed_ahead, ahead_kept, _ = norm(ahead_input[0], ahead_order, ahead_turn)
    ahead_near = along_y(normed_ahead)
    normed_back, back_kept, scales_back = norm(back_input[0], back_order, back_turn)
    back_near = along_y(after(normed_back, ahead_near, far_cotangent, far_order))

    ahead_far = cross(ahead_near)
    pairs, cotangent_kept = whole(
        pair_kernel,
        (table(2 * tokens, features), table(tokens, features)),
        after(back_cotangent[0], back_near),
        far_cotangent,
        back_order,
        far_order,
        back_turn,
    )
    back_far = cross(back_near, pairs, ahead_far)
    pairs = along_y(pairs)

    ahead_groups, back_groups = (2 * cap, 2 * cap), (2 * cap, cap, cap)
    wide = lambda dtype: pltpu.VMEM((2 * tokens, 2 * units), dtype)
    partials = through_expert(
        forward_kernel,
        place,
        (ahead_near, ahead_far),
        weights,
        (*ahead_groups, *ahead_groups),
        False,
        [wide(jnp.float32)] * 2 + [wide(jnp.bfloat16)] * 2,
    )
    ahead_home, ahead_away = partials[:2], partials[2:]
    partials = through_expert(
        backward_kernel,
        after(place, *ahead_home),
        (back_near, back_far, pairs),
        weights,
        (*back_groups, *back_groups),
        True,
        [wide(jnp.float32)] * 3 + [wide(jnp.bfloat16)] * 4,
    )
    back_home, back_away = partials[:3], partials[3:]

    def to_owner(home, other, *first):
        blocks = whole(sum_kernel, [table(cap, features)] * (home.shape[0] // cap), home, other)
        return blocks[-1], [move(b, dy=-k) for b, k in zip(blocks, first)]

    def in_turn(turn, values):
        chosen = lax.broadcasted_iota(jnp.int32, (tokens, tokens), 0) == turn
        return jnp.sum(jnp.where(chosen, values, 0.0), axis=1, keepdims=True)

    ahead_gates = in_turn(ahead_turn, ahead_gate)
    back_gates = in_turn(back_turn, back_gate)

    token = jnp.arange(tokens, dtype=jnp.float32)[None]
    ahead_rows = (ahead_kept, ahead_gates, in_turn(ahead_turn, token))
    back_rows = (back_kept, back_gates, in_turn(back_turn, token), cotangent_kept, scales_back)

    def finish_ahead(first, blocks, summed=False):
        rows = cap if summed else cap * len(blocks)
        kernel = functools.partial(ahead_kernel, first * cap, summed)
        return whole(kernel, table(rows, features + LANES), *ahead_rows, *blocks)

    def finish_back(first, blocks, summed=False):
        rows = cap if summed else cap * len(blocks)
        return whole(
            functools.partial(back_kernel, first * cap, summed),
            table(rows, features + LANES),
            *back_rows,
            *blocks,
            scratch=[pltpu.VMEM((rows, features), jnp.float32)],
        )


    a0 = cross(ahead_away[0])
    b0 = cross(back_away[0], a0)
    b1 = cross(back_away[1])
    done, asum = to_owner(after(ahead_home[0], back_home[0]), a0, *ORDER[:2])
    done, bsum = to_owner(after(back_home[0], done), b0, *ORDER[:2])
    done, bsum2 = to_owner(after(back_home[1], done), b1, *ORDER[2:3])
    a1 = cross(ahead_away[1], b0, b1)
    ahead_low = finish_ahead(0, [after(asum[0], done), asum[1]])
    zA13 = move(ahead_low, dpp=1)
    back_low = finish_back(0, [after(bsum[0], ahead_low), bsum[1]])
    zB13 = move(back_low, dpp=-1)
    b2 = cross(back_away[2], b1)
    done = finish_back(2, [after(bsum2[0], back_low)])
    zB2 = move(done, dpp=-1)
    ahead_sum, ahead_own = whole(sum_kernel, [table(cap, features)] * 2, after(ahead_home[1], done), a1)
    asum2 = [move(ahead_sum, dy=-ORDER[2])]
    done = finish_back(3, [after(back_home[2], ahead_own, zB13), b2], True)
    zB0 = move(done, dpp=-1)
    done = finish_ahead(2, [after(asum2[0], done, zA13, b2), ahead_own])
    zA2 = move(done, dpp=1)
    ahead_output = unpick([after(zA13, done), zA2], tokens, features)
    back_gradient = unpick([zB13, zB2, zB0], tokens, features)
    return (ahead_output[None], back_gradient[None])


def solution(mesh):
    placed = (
        P("pp", "ep", None),
        P("pp", "ep"),
        P("pp", "ep"),
        P("pp", "ep"),
        P("pp", "ep", None),
        P("pp", "ep", None),
        P("pp", "ep"),
        P("pp", "ep"),
        P("pp", "ep"),
        P("pp", "ep", None, None),
        P("pp", "ep", None, None),
        P("pp", "ep", None, None),
    )
    return jax.shard_map(
        body,
        mesh=mesh,
        in_specs=placed,
        out_specs=(P("pp", "ep", None), P("pp", "ep", None)),
        check_vma=False,
    )
```

```python
import functools

import jax
import jax.numpy as jnp
from jax import lax
from jax.experimental import pallas as pl
from jax.experimental.pallas import tpu as pltpu
from jax.sharding import PartitionSpec as P

EPSILON = 1e-06
NY, NX, NC = 4, 2, 2
ORDER = (1, 3, 2, 0)
WIDE = 1024
SPAN = 3584
LANES = 128
VMEM = pltpu.CompilerParams(vmem_limit_bytes=40 * 1024 * 1024)
LIGHT = pl.CostEstimate(flops=1000, bytes_accessed=1000, transcendentals=0)


def move(block, dpp=0, dy=0, dx=0, dc=0):
    npp = lax.axis_size("pp")
    nep = lax.axis_size("ep")
    route = []
    for r in range(npp):
        for y in range(NY):
            for x in range(NX):
                for c in range(NC):
                    source = r * nep + (y * NX + x) * NC + c
                    to = ((y + dy) % NY * NX + (x + dx) % NX) * NC + (c + dc) % NC
                    route.append((source, (r + dpp) % npp * nep + to))
    return lax.ppermute(block, ("pp", "ep"), route)


def after(value, *earlier):
    return lax.optimization_barrier((value, *earlier))[0]


def contract_last(left, right):
    return lax.dot_general(
        left, right, (((1,), (1,)), ((), ())), preferred_element_type=jnp.float32
    )


def dot(left, right):
    return jnp.dot(left, right, preferred_element_type=jnp.float32)


def one_hot(positions):
    n = positions.shape[-1]
    index = lax.broadcasted_iota(jnp.int32, (n, n), 0)
    return (index == positions).astype(jnp.bfloat16)


def whole(kernel, outs, *operands, scratch=()):
    return pl.pallas_call(
        kernel,
        out_shape=outs,
        in_specs=[pl.BlockSpec(memory_space=pltpu.SMEM if o.shape == (1,) else pltpu.VMEM) for o in operands],
        out_specs=jax.tree.map(lambda _: pl.BlockSpec(memory_space=pltpu.VMEM), outs),
        scratch_shapes=scratch,
        compiler_params=VMEM,
        cost_estimate=LIGHT,
    )(*operands)


def table(rows, features):
    return jax.ShapeDtypeStruct((rows, features), jnp.bfloat16)


def norm_kernel(inputs, expert_order, back_order, normed, kept, scales):
    features = inputs.shape[1]
    to_experts, to_back = one_hot(expert_order[...]), one_hot(back_order[...])
    sums = jnp.zeros((inputs.shape[0], 1), jnp.float32)
    kept_sums = sums
    for j in range(0, features, WIDE):
        values = inputs[:, j : j + WIDE]
        wide = values.astype(jnp.float32)
        sums += jnp.sum(wide * wide, axis=1, keepdims=True)
        moved = dot(to_back, values)
        kept_sums += jnp.sum(moved * moved, axis=1, keepdims=True)
        kept[:, j : j + WIDE] = moved.astype(jnp.bfloat16)
    scale = lax.rsqrt(sums / features + EPSILON)
    scales[...] = lax.rsqrt(kept_sums / features + EPSILON)
    for j in range(0, features, WIDE):
        scaled = (inputs[:, j : j + WIDE].astype(jnp.float32) * scale).astype(jnp.bfloat16)
        normed[:, j : j + WIDE] = dot(to_experts, scaled).astype(jnp.bfloat16)


def norm(inputs, expert_order, back_order):
    rows, features = inputs.shape
    outs = (table(rows, features), table(rows, features), jax.ShapeDtypeStruct((rows, 1), jnp.float32))
    return whole(norm_kernel, outs, inputs, expert_order, back_order)


def pair_kernel(near, far, near_order, far_order, back_order, pairs, kept):
    features = near.shape[1]
    cap = near.shape[0] // NY
    to_near, to_far, to_back = one_hot(near_order[...]), one_hot(far_order[...]), one_hot(back_order[...])
    for j in range(0, features, WIDE):
        here = slice(j, j + WIDE)
        kept[:, here] = dot(to_back, near[:, here]).astype(jnp.bfloat16)
        one = dot(to_near, near[:, here]).astype(jnp.bfloat16)
        two = dot(to_far, far[:, here]).astype(jnp.bfloat16)
        for e in range(NY):
            pairs[2 * e * cap : (2 * e + 1) * cap, here] = one[e * cap : (e + 1) * cap]
            pairs[(2 * e + 1) * cap : (2 * e + 2) * cap, here] = two[e * cap : (e + 1) * cap]


def unpick_kernel(*refs):
    *parts, out = refs
    tokens, features = out.shape

    def rows(here):
        return jnp.concatenate([p[:, here] for p in parts], axis=0)

    token = rows(slice(features, features + LANES)).astype(jnp.float32)
    index = lax.broadcasted_iota(jnp.int32, (tokens, LANES), 1).astype(jnp.float32)
    chosen = (token == index).astype(jnp.bfloat16).T
    for j in range(0, features, WIDE):
        here = slice(j, j + WIDE)
        out[:, here] = dot(chosen, rows(here)).astype(jnp.bfloat16)


def unpick(parts, tokens, features):
    return whole(unpick_kernel, table(tokens, features), *parts)


def sum_kernel(near, far, *outs):
    start = 0
    for out in outs:
        here = slice(start, start + out.shape[0])
        for j in range(0, out.shape[1], WIDE):
            across = slice(j, j + WIDE)
            total = near[here, across].astype(jnp.float32) + far[here, across].astype(jnp.float32)
            out[:, across] = total.astype(jnp.bfloat16)
        start += out.shape[0]


def read_total(blocks, summed, across):
    if not summed:
        return jnp.concatenate([b[:, across] for b in blocks], axis=0).astype(jnp.float32)
    return sum(b[:, across].astype(jnp.float32) for b in blocks)


def ahead_kernel(first, summed, kept, gates, tokens, *refs):
    *blocks, out = refs
    rows, features = out.shape[0], kept.shape[1]
    here = slice(first, first + rows)
    out[:, features:] = jnp.broadcast_to(tokens[here], (rows, LANES)).astype(jnp.bfloat16)
    for j in range(0, features, WIDE):
        across = slice(j, j + WIDE)
        total = read_total(blocks, summed, across)
        out[:, across] = (kept[here, across].astype(jnp.float32) + gates[here] * total).astype(jnp.bfloat16)


def back_kernel(first, summed, kept, gates, tokens, cotangent, scales, *refs):
    *blocks, out, grads = refs
    rows, features = out.shape[0], kept.shape[1]
    here = slice(first, first + rows)
    scale = scales[here]
    out[:, features:] = jnp.broadcast_to(tokens[here], (rows, LANES)).astype(jnp.bfloat16)
    inner_sum = jnp.zeros((rows, 1), jnp.float32)
    for j in range(0, features, WIDE):
        across = slice(j, j + WIDE)
        grad_normed = gates[here] * read_total(blocks, summed, across)
        grads[:, across] = grad_normed
        inner_sum += jnp.sum(grad_normed * kept[here, across].astype(jnp.float32), axis=1, keepdims=True)
    cubed = scale * scale * scale
    for j in range(0, features, WIDE):
        across = slice(j, j + WIDE)
        values = kept[here, across].astype(jnp.float32)
        grad_layer = (
            scale * grads[:, across]
            - cubed * values * inner_sum / features
            + cotangent[here, across].astype(jnp.float32)
        )
        out[:, across] = grad_layer.astype(jnp.bfloat16)


def by_distance(place, held, turned):
    half = held.shape[0] // 2
    cap = half // NY
    for h in range(2):
        for i, k in enumerate(ORDER):
            start = pl.multiple_of(h * half + (place[0] - k + NY) % NY * cap, cap)
            turned[h * half + i * cap : h * half + (i + 1) * cap] = held[pl.ds(start, cap)]


def store_parts(result, outs):
    start = 0
    for out in outs:
        out[...] = result[start : start + out.shape[0]].astype(jnp.bfloat16)
        start += out.shape[0]


def forward_kernel(steps, place, near, far, g0, g1, u0, u1, d0, d1, *refs):
    *outs, gated, lifted, hidden, turned = refs
    step = pl.program_id(0)
    half = g0.shape[1]

    @pl.when(step == 0)
    def _():
        gated[...] = jnp.zeros_like(gated)
        lifted[...] = jnp.zeros_like(lifted)

    @pl.when(step < steps)
    def _():
        rows = jnp.concatenate([near[...], far[...]], axis=0)
        gated[:, :half] += dot(rows, g0[...])
        gated[:, half:] += dot(rows, g1[...])
        lifted[:, :half] += dot(rows, u0[...])
        lifted[:, half:] += dot(rows, u1[...])

    @pl.when(step == steps - 1)
    def _():
        hidden[...] = (jax.nn.silu(gated[...]) * lifted[...]).astype(jnp.bfloat16)
        by_distance(place, hidden, turned)

    @pl.when(step >= steps)
    def _():
        store_parts(dot(turned[:, :half], d0[...]) + dot(turned[:, half:], d1[...]), outs)


def backward_kernel(steps, place, near, far, pairs, g0, g1, u0, u1, d0, d1, *refs):
    *outs, gated, lifted, upstream, gate_gradient, up_gradient, turned_gate, turned_up = refs
    step = pl.program_id(0)
    half = g0.shape[1]
    tokens = near.shape[0]
    cap = tokens // NY

    @pl.when(step == 0)
    def _():
        gated[...] = jnp.zeros_like(gated)
        lifted[...] = jnp.zeros_like(lifted)
        upstream[...] = jnp.zeros_like(upstream)

    @pl.when(step < steps)
    def _():
        rows = jnp.concatenate([near[...], far[...]], axis=0)
        gated[:, :half] += dot(rows, g0[...])
        gated[:, half:] += dot(rows, g1[...])
        lifted[:, :half] += dot(rows, u0[...])
        lifted[:, half:] += dot(rows, u1[...])
        upstream[:, :half] += contract_last(pairs[...], d0[...])
        upstream[:, half:] += contract_last(pairs[...], d1[...])

    @pl.when(step == steps - 1)
    def _():
        for h in range(2):
            for q in range(NY):
                here = slice(h * tokens + q * cap, h * tokens + (q + 1) * cap)
                gate, lift = gated[here], lifted[here]
                up = upstream[(2 * q + h) * cap : (2 * q + h + 1) * cap]
                sig = jax.nn.sigmoid(gate)
                gate_gradient[here] = (up * lift * sig * (1.0 + gate * (1.0 - sig))).astype(jnp.bfloat16)
                up_gradient[here] = (up * gate * sig).astype(jnp.bfloat16)
        by_distance(place, gate_gradient, turned_gate)
        by_distance(place, up_gradient, turned_up)

    @pl.when(step >= steps)
    def _():
        result = contract_last(turned_gate[:, :half], g0[...]) + contract_last(turned_gate[:, half:], g1[...])
        result += contract_last(turned_up[:, :half], u0[...]) + contract_last(turned_up[:, half:], u1[...])
        store_parts(result, outs)


def through_expert(kernel, place, rows, weights, parts, twice, scratch):
    features = rows[0].shape[1]
    steps = features // SPAN
    first = lambda i: jnp.minimum(i, steps - 1)
    second = lambda i: jnp.maximum(i - steps, 0)
    both = lambda i: i % steps
    gate = [pl.BlockSpec((SPAN, w.shape[1]), lambda i: ((both if twice else first)(i), 0)) for w in weights[:4]]
    down = [pl.BlockSpec((w.shape[0], SPAN), lambda i: (0, (first if twice else second)(i))) for w in weights[4:]]
    return pl.pallas_call(
        functools.partial(kernel, steps),
        grid=(2 * steps,),
        out_shape=[table(n, features) for n in parts],
        in_specs=[pl.BlockSpec(memory_space=pltpu.SMEM)]
        + [pl.BlockSpec((r.shape[0], SPAN), lambda i: (0, first(i))) for r in rows]
        + gate
        + down,
        out_specs=[pl.BlockSpec((n, SPAN), lambda i: (0, second(i))) for n in parts],
        scratch_shapes=scratch,
        compiler_params=VMEM,
        cost_estimate=LIGHT,
    )(place, *rows, *weights)


def body(
    ahead_input,
    ahead_expert,
    ahead_slot,
    ahead_gate,
    back_input,
    back_cotangent,
    back_expert,
    back_slot,
    back_gate,
    gate_weight,
    up_weight,
    down_weight,
):
    tokens, features = ahead_input.shape[1:]
    cap = tokens // NY
    units = gate_weight.shape[3]
    y = lax.axis_index("ep") // (NX * NC)
    place = y.astype(jnp.int32)[None]

    def along_y(rows):
        shape = (NY, rows.shape[0] // NY, features)
        groups = [
            [(q * NX + x) * NC + c for q in range(NY)] for x in range(NX) for c in range(NC)
        ]
        return lax.all_to_all(
            rows.reshape(shape), "ep", 0, 0, axis_index_groups=groups, tiled=True
        ).reshape(rows.shape)

    def cross(rows, *earlier):
        return move(after(rows, *earlier) if earlier else rows, dx=1)

    def positions(expert, slot):
        distance = (expert[0] - y + NY) % NY
        turn = jnp.select([distance == k for k in ORDER], list(range(NY)))
        return (expert * cap + slot), (turn * cap + slot[0])[None]

    ahead_order, ahead_turn = positions(ahead_expert, ahead_slot)
    back_order, back_turn = positions(back_expert, back_slot)
    half = tokens // 2

    far_cotangent = cross(back_cotangent[0])
    far_order = move(back_order, dx=1)
    gate_far = move(gate_weight[0, 0], dc=1)
    up_far = move(up_weight[0, 0], dc=1)
    down_far = move(down_weight[0, 0], dc=1)
    weights = (gate_weight[0, 0], gate_far, up_weight[0, 0], up_far, down_weight[0, 0], down_far)

    normed_ahead, ahead_kept, _ = norm(ahead_input[0], ahead_order, ahead_turn)
    ahead_near = along_y(normed_ahead)
    normed_back, back_kept, scales_back = norm(back_input[0], back_order, back_turn)
    back_near = along_y(after(normed_back, ahead_near, far_cotangent, far_order))

    ahead_far = cross(ahead_near)
    pairs, cotangent_kept = whole(
        pair_kernel,
        (table(2 * tokens, features), table(tokens, features)),
        after(back_cotangent[0], back_near),
        far_cotangent,
        back_order,
        far_order,
        back_turn,
    )
    back_far = cross(back_near)
    pairs = along_y(pairs)

    ahead_groups, back_groups = (2 * cap, 2 * cap), (2 * cap, cap, cap)
    wide = lambda dtype: pltpu.VMEM((2 * tokens, 2 * units), dtype)
    partials = through_expert(
        forward_kernel,
        place,
        (ahead_near, ahead_far),
        weights,
        (*ahead_groups, *ahead_groups),
        False,
        [wide(jnp.float32)] * 2 + [wide(jnp.bfloat16)] * 2,
    )
    ahead_home, ahead_away = partials[:2], partials[2:]
    partials = through_expert(
        backward_kernel,
        after(place, *ahead_home),
        (back_near, back_far, pairs),
        weights,
        (*back_groups, *back_groups),
        True,
        [wide(jnp.float32)] * 3 + [wide(jnp.bfloat16)] * 4,
    )
    back_home, back_away = partials[:3], partials[3:]

    def to_owner(home, other, *first):
        blocks = whole(sum_kernel, [table(cap, features)] * (home.shape[0] // cap), home, other)
        return blocks[-1], [move(b, dy=-k) for b, k in zip(blocks, first)]

    def in_turn(turn, values):
        chosen = lax.broadcasted_iota(jnp.int32, (tokens, tokens), 0) == turn
        return jnp.sum(jnp.where(chosen, values, 0.0), axis=1, keepdims=True)

    ahead_gates = in_turn(ahead_turn, ahead_gate)
    back_gates = in_turn(back_turn, back_gate)

    token = jnp.arange(tokens, dtype=jnp.float32)[None]
    ahead_rows = (ahead_kept, ahead_gates, in_turn(ahead_turn, token))
    back_rows = (back_kept, back_gates, in_turn(back_turn, token), cotangent_kept, scales_back)

    def finish_ahead(first, blocks, summed=False):
        rows = cap if summed else cap * len(blocks)
        kernel = functools.partial(ahead_kernel, first * cap, summed)
        return whole(kernel, table(rows, features + LANES), *ahead_rows, *blocks)

    def finish_back(first, blocks, summed=False):
        rows = cap if summed else cap * len(blocks)
        return whole(
            functools.partial(back_kernel, first * cap, summed),
            table(rows, features + LANES),
            *back_rows,
            *blocks,
            scratch=[pltpu.VMEM((rows, features), jnp.float32)],
        )


    a0 = cross(ahead_away[0])
    b0 = cross(back_away[0], a0)
    b1 = cross(back_away[1])
    done, asum = to_owner(after(ahead_home[0], back_home[0]), a0, *ORDER[:2])
    done, bsum = to_owner(after(back_home[0], done), b0, *ORDER[:2])
    done, bsum2 = to_owner(after(back_home[1], done), b1, *ORDER[2:3])
    a1 = cross(ahead_away[1], b0, b1)
    ahead_low = finish_ahead(0, [after(asum[0], done), asum[1]])
    zA13 = move(ahead_low, dpp=1)
    back_low = finish_back(0, [after(bsum[0], ahead_low), bsum[1]])
    zB13 = move(back_low, dpp=-1)
    b2 = cross(back_away[2], b1)
    done = finish_back(2, [after(bsum2[0], back_low)])
    zB2 = move(done, dpp=-1)
    ahead_sum, ahead_own = whole(sum_kernel, [table(cap, features)] * 2, after(ahead_home[1], done), a1)
    asum2 = [move(ahead_sum, dy=-ORDER[2])]
    done = finish_back(3, [after(back_home[2], ahead_own, zB13), b2], True)
    zB0 = move(done, dpp=-1)
    done = finish_ahead(2, [after(asum2[0], done, zA13, b2), ahead_own])
    zA2 = move(done, dpp=1)
    ahead_output = unpick([after(zA13, done), zA2], tokens, features)
    back_gradient = unpick([zB13, zB2, zB0], tokens, features)
    return (ahead_output[None], back_gradient[None])


def solution(mesh):
    placed = (
        P("pp", "ep", None),
        P("pp", "ep"),
        P("pp", "ep"),
        P("pp", "ep"),
        P("pp", "ep", None),
        P("pp", "ep", None),
        P("pp", "ep"),
        P("pp", "ep"),
        P("pp", "ep"),
        P("pp", "ep", None, None),
        P("pp", "ep", None, None),
        P("pp", "ep", None, None),
    )
    return jax.shard_map(
        body,
        mesh=mesh,
        in_specs=placed,
        out_specs=(P("pp", "ep", None), P("pp", "ep", None)),
        check_vma=False,
    )
```

```python
import functools

import jax
import jax.numpy as jnp
from jax import lax
from jax.experimental import pallas as pl
from jax.experimental.pallas import tpu as pltpu
from jax.sharding import PartitionSpec as P

EPSILON = 1e-06
NY, NX, NC = 4, 2, 2
ORDER = (1, 3, 2, 0)
WIDE = 1024
SPAN = 3584
LANES = 128
VMEM = pltpu.CompilerParams(vmem_limit_bytes=40 * 1024 * 1024)
LIGHT = pl.CostEstimate(flops=1000, bytes_accessed=1000, transcendentals=0)


def move(block, dpp=0, dy=0, dx=0, dc=0):
    npp = lax.axis_size("pp")
    nep = lax.axis_size("ep")
    route = []
    for r in range(npp):
        for y in range(NY):
            for x in range(NX):
                for c in range(NC):
                    source = r * nep + (y * NX + x) * NC + c
                    to = ((y + dy) % NY * NX + (x + dx) % NX) * NC + (c + dc) % NC
                    route.append((source, (r + dpp) % npp * nep + to))
    return lax.ppermute(block, ("pp", "ep"), route)


def after(value, *earlier):
    return lax.optimization_barrier((value, *earlier))[0]


def contract_last(left, right):
    return lax.dot_general(
        left, right, (((1,), (1,)), ((), ())), preferred_element_type=jnp.float32
    )


def dot(left, right):
    return jnp.dot(left, right, preferred_element_type=jnp.float32)


def one_hot(positions):
    n = positions.shape[-1]
    index = lax.broadcasted_iota(jnp.int32, (n, n), 0)
    return (index == positions).astype(jnp.bfloat16)


def whole(kernel, outs, *operands, scratch=()):
    return pl.pallas_call(
        kernel,
        out_shape=outs,
        in_specs=[pl.BlockSpec(memory_space=pltpu.SMEM if o.shape == (1,) else pltpu.VMEM) for o in operands],
        out_specs=jax.tree.map(lambda _: pl.BlockSpec(memory_space=pltpu.VMEM), outs),
        scratch_shapes=scratch,
        compiler_params=VMEM,
        cost_estimate=LIGHT,
    )(*operands)


def table(rows, features):
    return jax.ShapeDtypeStruct((rows, features), jnp.bfloat16)


def norm_kernel(inputs, expert_order, back_order, normed, kept, scales):
    features = inputs.shape[1]
    to_experts, to_back = one_hot(expert_order[...]), one_hot(back_order[...])
    sums = jnp.zeros((inputs.shape[0], 1), jnp.float32)
    kept_sums = sums
    for j in range(0, features, WIDE):
        values = inputs[:, j : j + WIDE]
        wide = values.astype(jnp.float32)
        sums += jnp.sum(wide * wide, axis=1, keepdims=True)
        moved = dot(to_back, values)
        kept_sums += jnp.sum(moved * moved, axis=1, keepdims=True)
        kept[:, j : j + WIDE] = moved.astype(jnp.bfloat16)
    scale = lax.rsqrt(sums / features + EPSILON)
    scales[...] = lax.rsqrt(kept_sums / features + EPSILON)
    for j in range(0, features, WIDE):
        scaled = (inputs[:, j : j + WIDE].astype(jnp.float32) * scale).astype(jnp.bfloat16)
        normed[:, j : j + WIDE] = dot(to_experts, scaled).astype(jnp.bfloat16)


def norm(inputs, expert_order, back_order):
    rows, features = inputs.shape
    outs = (table(rows, features), table(rows, features), jax.ShapeDtypeStruct((rows, 1), jnp.float32))
    return whole(norm_kernel, outs, inputs, expert_order, back_order)


def pair_kernel(near, far, near_order, far_order, back_order, pairs, kept):
    features = near.shape[1]
    cap = near.shape[0] // NY
    to_near, to_far, to_back = one_hot(near_order[...]), one_hot(far_order[...]), one_hot(back_order[...])
    for j in range(0, features, WIDE):
        here = slice(j, j + WIDE)
        kept[:, here] = dot(to_back, near[:, here]).astype(jnp.bfloat16)
        one = dot(to_near, near[:, here]).astype(jnp.bfloat16)
        two = dot(to_far, far[:, here]).astype(jnp.bfloat16)
        for e in range(NY):
            pairs[2 * e * cap : (2 * e + 1) * cap, here] = one[e * cap : (e + 1) * cap]
            pairs[(2 * e + 1) * cap : (2 * e + 2) * cap, here] = two[e * cap : (e + 1) * cap]


def unpick_kernel(*refs):
    *parts, out = refs
    names, parts = parts[: len(parts) // 2], parts[len(parts) // 2 :]
    token = jnp.concatenate([p[...] for p in names], axis=0).astype(jnp.float32)
    index = lax.broadcasted_iota(jnp.int32, token.shape, 1).astype(jnp.float32)
    chosen = (token == index).astype(jnp.bfloat16).T
    rows = jnp.concatenate([p[...] for p in parts], axis=0)
    out[...] = dot(chosen, rows).astype(jnp.bfloat16)


def unpick(parts, tokens, features):
    across = features // 4
    return pl.pallas_call(
        unpick_kernel,
        grid=(4,),
        out_shape=table(tokens, features),
        in_specs=[pl.BlockSpec((p.shape[0], LANES), lambda i: (0, features // LANES)) for p in parts]
        + [pl.BlockSpec((p.shape[0], across), lambda i: (0, i)) for p in parts],
        out_specs=pl.BlockSpec((tokens, across), lambda i: (0, i)),
        compiler_params=VMEM,
        cost_estimate=LIGHT,
    )(*parts, *parts)


def sum_kernel(near, far, *outs):
    start = 0
    for out in outs:
        here = slice(start, start + out.shape[0])
        for j in range(0, out.shape[1], WIDE):
            across = slice(j, j + WIDE)
            total = near[here, across].astype(jnp.float32) + far[here, across].astype(jnp.float32)
            out[:, across] = total.astype(jnp.bfloat16)
        start += out.shape[0]


def read_total(blocks, summed, across):
    if not summed:
        return jnp.concatenate([b[:, across] for b in blocks], axis=0).astype(jnp.float32)
    return sum(b[:, across].astype(jnp.float32) for b in blocks)


def ahead_kernel(first, summed, kept, gates, tokens, *refs):
    *blocks, out = refs
    rows, features = out.shape[0], kept.shape[1]
    here = slice(first, first + rows)
    out[:, features:] = jnp.broadcast_to(tokens[here], (rows, LANES)).astype(jnp.bfloat16)
    for j in range(0, features, WIDE):
        across = slice(j, j + WIDE)
        total = read_total(blocks, summed, across)
        out[:, across] = (kept[here, across].astype(jnp.float32) + gates[here] * total).astype(jnp.bfloat16)


def back_kernel(first, summed, kept, gates, tokens, cotangent, scales, *refs):
    *blocks, out, grads = refs
    rows, features = out.shape[0], kept.shape[1]
    here = slice(first, first + rows)
    scale = scales[here]
    out[:, features:] = jnp.broadcast_to(tokens[here], (rows, LANES)).astype(jnp.bfloat16)
    inner_sum = jnp.zeros((rows, 1), jnp.float32)
    for j in range(0, features, WIDE):
        across = slice(j, j + WIDE)
        grad_normed = gates[here] * read_total(blocks, summed, across)
        grads[:, across] = grad_normed
        inner_sum += jnp.sum(grad_normed * kept[here, across].astype(jnp.float32), axis=1, keepdims=True)
    cubed = scale * scale * scale
    for j in range(0, features, WIDE):
        across = slice(j, j + WIDE)
        values = kept[here, across].astype(jnp.float32)
        grad_layer = (
            scale * grads[:, across]
            - cubed * values * inner_sum / features
            + cotangent[here, across].astype(jnp.float32)
        )
        out[:, across] = grad_layer.astype(jnp.bfloat16)


def by_distance(place, held, turned):
    half = held.shape[0] // 2
    cap = half // NY
    for h in range(2):
        for i, k in enumerate(ORDER):
            start = pl.multiple_of(h * half + (place[0] - k + NY) % NY * cap, cap)
            turned[h * half + i * cap : h * half + (i + 1) * cap] = held[pl.ds(start, cap)]


def store_parts(result, outs):
    start = 0
    for out in outs:
        out[...] = result[start : start + out.shape[0]].astype(jnp.bfloat16)
        start += out.shape[0]


def forward_kernel(steps, place, near, far, g0, g1, u0, u1, d0, d1, *refs):
    *outs, gated, lifted, hidden, turned = refs
    step = pl.program_id(0)
    half = g0.shape[1]

    @pl.when(step == 0)
    def _():
        gated[...] = jnp.zeros_like(gated)
        lifted[...] = jnp.zeros_like(lifted)

    @pl.when(step < steps)
    def _():
        rows = jnp.concatenate([near[...], far[...]], axis=0)
        gated[:, :half] += dot(rows, g0[...])
        gated[:, half:] += dot(rows, g1[...])
        lifted[:, :half] += dot(rows, u0[...])
        lifted[:, half:] += dot(rows, u1[...])

    @pl.when(step == steps - 1)
    def _():
        hidden[...] = (jax.nn.silu(gated[...]) * lifted[...]).astype(jnp.bfloat16)
        by_distance(place, hidden, turned)

    @pl.when(step >= steps)
    def _():
        store_parts(dot(turned[:, :half], d0[...]) + dot(turned[:, half:], d1[...]), outs)


def backward_kernel(steps, place, near, far, pairs, g0, g1, u0, u1, d0, d1, *refs):
    *outs, gated, lifted, upstream, gate_gradient, up_gradient, turned_gate, turned_up = refs
    step = pl.program_id(0)
    half = g0.shape[1]
    tokens = near.shape[0]
    cap = tokens // NY

    @pl.when(step == 0)
    def _():
        gated[...] = jnp.zeros_like(gated)
        lifted[...] = jnp.zeros_like(lifted)
        upstream[...] = jnp.zeros_like(upstream)

    @pl.when(step < steps)
    def _():
        rows = jnp.concatenate([near[...], far[...]], axis=0)
        gated[:, :half] += dot(rows, g0[...])
        gated[:, half:] += dot(rows, g1[...])
        lifted[:, :half] += dot(rows, u0[...])
        lifted[:, half:] += dot(rows, u1[...])
        upstream[:, :half] += contract_last(pairs[...], d0[...])
        upstream[:, half:] += contract_last(pairs[...], d1[...])

    @pl.when(step == steps - 1)
    def _():
        for h in range(2):
            for q in range(NY):
                here = slice(h * tokens + q * cap, h * tokens + (q + 1) * cap)
                gate, lift = gated[here], lifted[here]
                up = upstream[(2 * q + h) * cap : (2 * q + h + 1) * cap]
                sig = jax.nn.sigmoid(gate)
                gate_gradient[here] = (up * lift * sig * (1.0 + gate * (1.0 - sig))).astype(jnp.bfloat16)
                up_gradient[here] = (up * gate * sig).astype(jnp.bfloat16)
        by_distance(place, gate_gradient, turned_gate)
        by_distance(place, up_gradient, turned_up)

    @pl.when(step >= steps)
    def _():
        result = contract_last(turned_gate[:, :half], g0[...]) + contract_last(turned_gate[:, half:], g1[...])
        result += contract_last(turned_up[:, :half], u0[...]) + contract_last(turned_up[:, half:], u1[...])
        store_parts(result, outs)


def through_expert(kernel, place, rows, weights, parts, twice, scratch):
    features = rows[0].shape[1]
    steps = features // SPAN
    first = lambda i: jnp.minimum(i, steps - 1)
    second = lambda i: jnp.maximum(i - steps, 0)
    both = lambda i: i % steps
    gate = [pl.BlockSpec((SPAN, w.shape[1]), lambda i: ((both if twice else first)(i), 0)) for w in weights[:4]]
    down = [pl.BlockSpec((w.shape[0], SPAN), lambda i: (0, (first if twice else second)(i))) for w in weights[4:]]
    return pl.pallas_call(
        functools.partial(kernel, steps),
        grid=(2 * steps,),
        out_shape=[table(n, features) for n in parts],
        in_specs=[pl.BlockSpec(memory_space=pltpu.SMEM)]
        + [pl.BlockSpec((r.shape[0], SPAN), lambda i: (0, first(i))) for r in rows]
        + gate
        + down,
        out_specs=[pl.BlockSpec((n, SPAN), lambda i: (0, second(i))) for n in parts],
        scratch_shapes=scratch,
        compiler_params=VMEM,
        cost_estimate=LIGHT,
    )(place, *rows, *weights)


def body(
    ahead_input,
    ahead_expert,
    ahead_slot,
    ahead_gate,
    back_input,
    back_cotangent,
    back_expert,
    back_slot,
    back_gate,
    gate_weight,
    up_weight,
    down_weight,
):
    tokens, features = ahead_input.shape[1:]
    cap = tokens // NY
    units = gate_weight.shape[3]
    y = lax.axis_index("ep") // (NX * NC)
    place = y.astype(jnp.int32)[None]

    def along_y(rows):
        shape = (NY, rows.shape[0] // NY, features)
        groups = [
            [(q * NX + x) * NC + c for q in range(NY)] for x in range(NX) for c in range(NC)
        ]
        return lax.all_to_all(
            rows.reshape(shape), "ep", 0, 0, axis_index_groups=groups, tiled=True
        ).reshape(rows.shape)

    def cross(rows, *earlier):
        return move(after(rows, *earlier) if earlier else rows, dx=1)

    def positions(expert, slot):
        distance = (expert[0] - y + NY) % NY
        turn = jnp.select([distance == k for k in ORDER], list(range(NY)))
        return (expert * cap + slot), (turn * cap + slot[0])[None]

    ahead_order, ahead_turn = positions(ahead_expert, ahead_slot)
    back_order, back_turn = positions(back_expert, back_slot)
    half = tokens // 2

    far_cotangent = cross(back_cotangent[0])
    far_order = move(back_order, dx=1)
    gate_far = move(gate_weight[0, 0], dc=1)
    up_far = move(up_weight[0, 0], dc=1)
    down_far = move(down_weight[0, 0], dc=1)
    weights = (gate_weight[0, 0], gate_far, up_weight[0, 0], up_far, down_weight[0, 0], down_far)

    normed_ahead, ahead_kept, _ = norm(ahead_input[0], ahead_order, ahead_turn)
    ahead_near = along_y(normed_ahead)
    normed_back, back_kept, scales_back = norm(back_input[0], back_order, back_turn)
    back_near = along_y(after(normed_back, ahead_near, far_cotangent, far_order))

    ahead_far = cross(ahead_near)
    pairs, cotangent_kept = whole(
        pair_kernel,
        (table(2 * tokens, features), table(tokens, features)),
        after(back_cotangent[0], back_near),
        far_cotangent,
        back_order,
        far_order,
        back_turn,
    )
    back_far = cross(back_near)
    pairs = along_y(pairs)

    ahead_groups, back_groups = (2 * cap, 2 * cap), (2 * cap, cap, cap)
    wide = lambda dtype: pltpu.VMEM((2 * tokens, 2 * units), dtype)
    partials = through_expert(
        forward_kernel,
        place,
        (ahead_near, ahead_far),
        weights,
        (*ahead_groups, *ahead_groups),
        False,
        [wide(jnp.float32)] * 2 + [wide(jnp.bfloat16)] * 2,
    )
    ahead_home, ahead_away = partials[:2], partials[2:]
    partials = through_expert(
        backward_kernel,
        after(place, *ahead_home),
        (back_near, back_far, pairs),
        weights,
        (*back_groups, *back_groups),
        True,
        [wide(jnp.float32)] * 3 + [wide(jnp.bfloat16)] * 4,
    )
    back_home, back_away = partials[:3], partials[3:]

    def to_owner(home, other, *first):
        blocks = whole(sum_kernel, [table(cap, features)] * (home.shape[0] // cap), home, other)
        return blocks[-1], [move(b, dy=-k) for b, k in zip(blocks, first)]

    def in_turn(turn, values):
        chosen = lax.broadcasted_iota(jnp.int32, (tokens, tokens), 0) == turn
        return jnp.sum(jnp.where(chosen, values, 0.0), axis=1, keepdims=True)

    ahead_gates = in_turn(ahead_turn, ahead_gate)
    back_gates = in_turn(back_turn, back_gate)

    token = jnp.arange(tokens, dtype=jnp.float32)[None]
    ahead_rows = (ahead_kept, ahead_gates, in_turn(ahead_turn, token))
    back_rows = (back_kept, back_gates, in_turn(back_turn, token), cotangent_kept, scales_back)

    def finish_ahead(first, blocks, summed=False):
        rows = cap if summed else cap * len(blocks)
        kernel = functools.partial(ahead_kernel, first * cap, summed)
        return whole(kernel, table(rows, features + LANES), *ahead_rows, *blocks)

    def finish_back(first, blocks, summed=False):
        rows = cap if summed else cap * len(blocks)
        return whole(
            functools.partial(back_kernel, first * cap, summed),
            table(rows, features + LANES),
            *back_rows,
            *blocks,
            scratch=[pltpu.VMEM((rows, features), jnp.float32)],
        )


    a0 = cross(ahead_away[0])
    b0 = cross(back_away[0], a0)
    b1 = cross(back_away[1])
    done, asum = to_owner(after(ahead_home[0], back_home[0]), a0, *ORDER[:2])
    done, bsum = to_owner(after(back_home[0], done), b0, *ORDER[:2])
    done, bsum2 = to_owner(after(back_home[1], done), b1, *ORDER[2:3])
    a1 = cross(ahead_away[1], b0, b1)
    ahead_low = finish_ahead(0, [after(asum[0], done), asum[1]])
    zA13 = move(ahead_low, dpp=1)
    back_low = finish_back(0, [after(bsum[0], ahead_low), bsum[1]])
    zB13 = move(back_low, dpp=-1)
    b2 = cross(back_away[2], b1)
    done = finish_back(2, [after(bsum2[0], back_low)])
    zB2 = move(done, dpp=-1)
    ahead_sum, ahead_own = whole(sum_kernel, [table(cap, features)] * 2, after(ahead_home[1], done), a1)
    asum2 = [move(ahead_sum, dy=-ORDER[2])]
    done = finish_back(3, [after(back_home[2], ahead_own, zB13), b2], True)
    zB0 = move(done, dpp=-1)
    done = finish_ahead(2, [after(asum2[0], done, zA13, b2), ahead_own])
    zA2 = move(done, dpp=1)
    ahead_output = unpick([after(zA13, done), zA2], tokens, features)
    back_gradient = unpick([zB13, zB2, zB0], tokens, features)
    return (ahead_output[None], back_gradient[None])


def solution(mesh):
    placed = (
        P("pp", "ep", None),
        P("pp", "ep"),
        P("pp", "ep"),
        P("pp", "ep"),
        P("pp", "ep", None),
        P("pp", "ep", None),
        P("pp", "ep"),
        P("pp", "ep"),
        P("pp", "ep"),
        P("pp", "ep", None, None),
        P("pp", "ep", None, None),
        P("pp", "ep", None, None),
    )
    return jax.shard_map(
        body,
        mesh=mesh,
        in_specs=placed,
        out_specs=(P("pp", "ep", None), P("pp", "ep", None)),
        check_vma=False,
    )
```
